32 devices in a mesh: grp: 1, gx: 32 (over z, y, x, core).
Axes of the slice: x: 2, y: 2, z: 4, core: 2. Of those that a mesh axis runs over, the one named last changes fastest.
Arguments:
- out_grad: bfloat16 [16384, 768], P(('grp', 'gx')), may hold values from -6 to 6
- inputs: bfloat16 [16384, 768], P(('grp', 'gx')), may hold values from -6 to 6
- preact: bfloat16 [16384, 3072], P(('grp', 'gx')), may hold values from -6 to 6
- w_out: bfloat16 [3072, 768], P('gx'), may hold values from -0.109375 to 0.109375
- w_in: bfloat16 [768, 3072], P('gx'), may hold values from -0.21875 to 0.21875
Outputs:
- input_grad: float32 [16384, 768], P(('grp', 'gx'))
- w_out_grad: float32 [3072, 768], P(('grp', 'gx'))
- w_in_grad: float32 [768, 3072], P(('grp', 'gx'))
The draws below stay inside these ranges and needn't reach their ends.
All inputs are finite; a program needn't handle non-finite values.
Results may differ from the reference program's by a relative error of at most 0.0029.
Values may be sent and summed in bfloat16 or wider, within the bound.
No kernel may reach another device: no remote copies, remote signals or barrier semaphores. Data moves between devices by JAX's collectives and lax.ppermute only.
A program may use at most 128 MiB of HBM per device.

```python
import math
import jax
import jax.numpy as jnp

DT = 768
FT = 3072
TOKENS = 16384


def with_spikes(array, stream_key, source, target, parts, factor):
    def block_of(axis_at):
        return (jnp.arange(array.shape[axis_at]) // (array.shape[axis_at] // parts)).reshape((-1,) + (1,) * (array.ndim - 1 - axis_at))

    one_side = jax.random.permutation(stream_key, parts)[block_of(target)]
    other_side = (block_of(target) + parts // 2) % parts
    return jnp.where((block_of(source) == one_side) | (block_of(source) == other_side), factor * array, array)


def levels(stream_key, dims, split, least, high):
    gain = 1.0
    for position, parts in split:
        steps = jax.random.uniform(jax.random.fold_in(jax.random.fold_in(stream_key, 6), position), (parts,), jnp.float32, least / len(split), high / len(split))
        gain = gain * jnp.repeat(jnp.exp(steps), dims[position] // parts).reshape((-1,) + (1,) * (len(dims) - 1 - position))
    return gain


def gaussian(own_key, dims, scale, reach, split=(), kind=jnp.bfloat16):
    drawn = jax.random.normal(own_key, dims, jnp.float32) * scale
    if len(split) > 0:
        drawn = levels(own_key, dims, split, -0.22, 0.18) * drawn
    return jnp.clip(drawn, min=-reach, max=reach).astype(kind)


def gaussian_with(key, shape, width, most, split, heavy, dtype=jnp.bfloat16):
    array = width * jax.random.normal(key, shape, jnp.float32)
    if split:
        array = array * levels(key, shape, split, -0.22, 0.18)
    return jnp.clip(with_spikes(array, jax.random.fold_in(key, 3), *heavy), -most, most).astype(dtype)


def setup_inputs(seed: int = 0, part: int = 0) -> dict:
    streams_of = jax.random.split(jax.random.key(seed), 6)
    own_keys = jax.random.split(jax.random.fold_in(streams_of[5], part), 6)
    out_grad = gaussian(own_keys[0], (TOKENS, DT), 1.0, 6.0, ((0, 32),))
    inputs = gaussian_with(own_keys[1], (TOKENS, DT), 1.0, 6.0, ((0, 32),), (0, 1, 32, 2.75))
    preact = gaussian_with(own_keys[2], (TOKENS, FT), 1.0, 6.0, ((0, 32),), (0, 1, 32, 2.75))
    w_out = gaussian(streams_of[3], (FT, DT), FT ** -0.5, 0.109375, ((0, 32),))
    w_in = gaussian(streams_of[4], (DT, FT), DT ** -0.5, 0.21875, ((0, 32),))
    return dict(out_grad=out_grad, inputs=inputs, preact=preact, w_out=w_out, w_in=w_in)


def gelu_parts(preact):
    value = preact.astype(jnp.float32)
    coeff = math.sqrt(2.0 / math.pi)
    inner = coeff * (value + 0.044715 * value * value * value)
    tangent = jnp.tanh(inner)
    activ = 0.5 * value * (1.0 + tangent)
    gelu_slope = 0.5 * (1.0 + tangent) + 0.5 * value * (1.0 - tangent * tangent) * coeff * (1.0 + 3.0 * 0.044715 * value * value)
    return (activ.astype(jnp.bfloat16), gelu_slope)

def reference(out_grad, inputs, preact, w_out, w_in):
    activ, gelu_slope = gelu_parts(preact)
    act_grad = jnp.dot(out_grad, w_out.T, preferred_element_type=jnp.float32)
    pre_grad = (act_grad * gelu_slope).astype(jnp.bfloat16)
    input_grad = jnp.dot(pre_grad, w_in.T, preferred_element_type=jnp.float32)
    grad_scale = 1.0 / math.sqrt(TOKENS)
    w_out_grad = jnp.dot(activ.T, out_grad, preferred_element_type=jnp.float32) * grad_scale
    w_in_grad = jnp.dot(inputs.T, pre_grad, preferred_element_type=jnp.float32) * grad_scale
    return (input_grad, w_out_grad, w_in_grad)
```

```python
import math

import jax
import jax.numpy as jnp
from jax import lax
from jax.sharding import PartitionSpec as P

AXIS = "gx"
BF = jnp.bfloat16
F32 = jnp.float32


def gelu_parts(preact):
    value = preact.astype(F32)
    coeff = math.sqrt(2.0 / math.pi)
    inner = coeff * (value + 0.044715 * value * value * value)
    tangent = jnp.tanh(inner)
    activ = 0.5 * value * (1.0 + tangent)
    gelu_slope = 0.5 * (1.0 + tangent) + 0.5 * value * (1.0 - tangent * tangent) * coeff * (
        1.0 + 3.0 * 0.044715 * value * value
    )
    return (activ.astype(BF), gelu_slope)


def contract_last(left, right):
    return lax.dot_general(
        left, right, (((1,), (1,)), ((), ())), preferred_element_type=F32
    )


def contract_first(left, right):
    return lax.dot_general(
        left, right, (((0,), (0,)), ((), ())), preferred_element_type=F32
    )


def coords(d):
    return d // 8, (d // 4) % 2, (d // 2) % 2, d % 2


def index(z, y, x, c):
    return ((z * 2 + y) * 2 + x) * 2 + c


def moved(n, f):
    return [(d, index(*f(*coords(d)))) for d in range(n)]


def pick(array, at, axis):
    return lax.dynamic_index_in_dim(array, at, axis, keepdims=False)


def paired(mine, other, at, axis):
    first = jnp.where(at == 0, mine, other)
    second = jnp.where(at == 0, other, mine)
    return jnp.stack([first, second], axis)


def per_device(out_grad, inputs, preact, w_out, w_in):
    n = lax.axis_size(AXIS)
    nz = n // 8
    nl = nz // 2
    me = lax.axis_index(AXIS)
    z, y, x, c = coords(me)
    high, low = z // nl, z % nl
    grad_scale = 1.0 / math.sqrt(out_grad.shape[0] * n)
    tokens, width = out_grad.shape
    hidden = preact.shape[1]
    half = hidden // 2
    rows_out, rows_in = w_out.shape[0], w_in.shape[0]

    along_x = moved(n, lambda z, y, x, c: (z, y, 1 - x, c))
    along_y = moved(n, lambda z, y, x, c: (z, 1 - y, x, c))
    cores = moved(n, lambda z, y, x, c: (z, y, x, 1 - c))

    def send(array, perm):
        return lax.ppermute(array, AXIS, perm)

    def z_perm(k):
        return moved(n, lambda z, y, x, c: (z ^ k, y, x, c))

    def gather_perm(i, j):
        return moved(
            n, lambda z, y, x, c: ((c ^ i) * nl + ((z % nl) ^ j), y, x, z // nl)
        )

    def scatter_perm(i, j):
        return moved(
            n, lambda z, y, x, c: (c * nl + ((z % nl) ^ j), y, x, (z // nl) ^ i)
        )

    pre_split = preact.reshape(tokens, 2, half)
    pre_mine = pick(pre_split, c, 1)
    pre_other = send(pick(pre_split, 1 - c, 1), cores)
    out_grad2 = jnp.concatenate([out_grad, send(out_grad, cores)], 0)
    inputs2 = jnp.concatenate([inputs, send(inputs, cores)], 0)
    pre2 = jnp.concatenate([pre_mine, pre_other], 0)

    parts = [[send(w_out, gather_perm(i, j)) for j in range(nl)] for i in range(2)]
    parts = jnp.stack([jnp.stack(p, 0) for p in parts], 0)
    by_z = jnp.stack(
        [
            jnp.stack([parts[cc ^ high, ll ^ low] for cc in range(2)], 0)
            for ll in range(nl)
        ],
        0,
    )

    def gather_plane(array, cut):
        one, two = jnp.split(array, 2, cut)
        one = paired(one, send(one, along_x), x, 0)
        two = paired(two, send(two, along_y), y, 0)
        one = paired(one, send(one, along_y), y, 0)
        two = paired(two, send(two, along_x), x, 1)
        return jnp.concatenate([one, two], cut + 2)

    w_out2 = gather_plane(by_z, 1).transpose(2, 0, 1, 3, 4, 5).reshape(half, width)

    in_split = w_in.reshape(rows_in, 2, half)
    in_two = paired(pick(in_split, c, 1), send(pick(in_split, 1 - c, 1), cores), c, 0)
    parts = jnp.stack([in_two] + [send(in_two, z_perm(k)) for k in range(1, nz)], 0)
    by_z = jnp.stack([parts[zz ^ z] for zz in range(nz)], 0)
    w_in2 = gather_plane(by_z, 3).transpose(2, 0, 1, 3, 4, 5).reshape(width, half)

    def scatter_plane(total, cut):
        one, two = jnp.split(total, 2, cut)
        one = pick(one, x, 2) + send(pick(one, 1 - x, 2).astype(BF), along_x).astype(F32)
        two = pick(two, y, 1) + send(pick(two, 1 - y, 1).astype(BF), along_y).astype(F32)
        one = pick(one, y, 1) + send(pick(one, 1 - y, 1).astype(BF), along_y).astype(F32)
        two = pick(two, x, 1) + send(pick(two, 1 - x, 1).astype(BF), along_x).astype(F32)
        return jnp.concatenate([one, two], cut - 2)

    activ, slope = gelu_parts(pre2)
    total = contract_first(activ, out_grad2)
    total = total.reshape(nl, 2, 2, 2, rows_out, width)
    total = scatter_plane(total, 3)
    narrow = total.astype(BF)
    w_out_grad = 0.0
    for i in range(2):
        for j in range(nl):
            sent = send(narrow[low ^ j, high ^ i], scatter_perm(i, j)).astype(F32)
            if i == 0 and j == 0:
                sent = jnp.where(c == high, total[low, high], sent)
            w_out_grad = w_out_grad + sent
    w_out_grad = w_out_grad * grad_scale

    act_grad = contract_last(out_grad2, w_out2)
    pre_grad = (act_grad * slope).astype(BF)

    total = contract_first(inputs2, pre_grad)
    total = total.reshape(nz, 2, 2, 2 * rows_in, half)
    total = scatter_plane(total, 4)
    narrow = total.astype(BF)
    own = total[z]
    for k in range(1, nz):
        own = own + send(narrow[z ^ k], z_perm(k)).astype(F32)
    own = (own * grad_scale).reshape(2, rows_in, half)
    w_in_grad = paired(own[c], send(own[1 - c], cores), c, 1).reshape(rows_in, hidden)

    part = contract_last(pre_grad, w_in2)
    input_grad = part[:tokens] + send(part[tokens:], cores)
    return (input_grad, w_out_grad, w_in_grad)


def solution(mesh):
    in_specs = (
        P(("grp", "gx"), None),
        P(("grp", "gx"), None),
        P(("grp", "gx"), None),
        P("gx", None),
        P("gx", None),
    )
    out_specs = (P(("grp", "gx"), None), P(("grp", "gx"), None), P(("grp", "gx"), None))
    return jax.shard_map(
        per_device, mesh=mesh, in_specs=in_specs, out_specs=out_specs, check_vma=False
    )
```

```python
import math

import jax
import jax.numpy as jnp
from jax import lax
from jax.experimental import pallas as pl
from jax.experimental.pallas import tpu as pltpu
from jax.sharding import PartitionSpec as P

AXIS = "gx"
BF = jnp.bfloat16
F32 = jnp.float32


def gelu_parts(preact):
    value = preact.astype(F32)
    coeff = math.sqrt(2.0 / math.pi)
    inner = coeff * (value + 0.044715 * value * value * value)
    tangent = jnp.tanh(inner)
    activ = 0.5 * value * (1.0 + tangent)
    gelu_slope = 0.5 * (1.0 + tangent) + 0.5 * value * (1.0 - tangent * tangent) * coeff * (
        1.0 + 3.0 * 0.044715 * value * value
    )
    return (activ.astype(BF), gelu_slope)


def contract_last(left, right):
    return lax.dot_general(
        left, right, (((1,), (1,)), ((), ())), preferred_element_type=F32
    )


def contract_first(left, right):
    return lax.dot_general(
        left, right, (((0,), (0,)), ((), ())), preferred_element_type=F32
    )


def coords(d):
    return d // 8, (d // 4) % 2, (d // 2) % 2, d % 2


def index(z, y, x, c):
    return ((z * 2 + y) * 2 + x) * 2 + c


def moved(n, f):
    return [(d, index(*f(*coords(d)))) for d in range(n)]


def pick(array, at, axis):
    return lax.dynamic_index_in_dim(array, at, axis, keepdims=False)


def paired(mine, other, at, axis):
    first = jnp.where(at == 0, mine, other)
    second = jnp.where(at == 0, other, mine)
    return jnp.stack([first, second], axis)


def plain(out_grad, inputs, preact, w_out, w_in):
    n = lax.axis_size(AXIS)
    nz = n // 8
    nl = nz // 2
    me = lax.axis_index(AXIS)
    z, y, x, c = coords(me)
    high, low = z // nl, z % nl
    grad_scale = 1.0 / math.sqrt(out_grad.shape[0] * n)
    tokens, width = out_grad.shape
    hidden = preact.shape[1]
    half = hidden // 2
    rows_out, rows_in = w_out.shape[0], w_in.shape[0]

    along_x = moved(n, lambda z, y, x, c: (z, y, 1 - x, c))
    along_y = moved(n, lambda z, y, x, c: (z, 1 - y, x, c))
    cores = moved(n, lambda z, y, x, c: (z, y, x, 1 - c))

    def send(array, perm):
        return lax.ppermute(array, AXIS, perm)

    def z_perm(k):
        return moved(n, lambda z, y, x, c: (z ^ k, y, x, c))

    def gather_perm(i, j):
        return moved(
            n, lambda z, y, x, c: ((c ^ i) * nl + ((z % nl) ^ j), y, x, z // nl)
        )

    def scatter_perm(i, j):
        return moved(
            n, lambda z, y, x, c: (c * nl + ((z % nl) ^ j), y, x, (z // nl) ^ i)
        )

    pre_split = preact.reshape(tokens, 2, half)
    pre_mine = pick(pre_split, c, 1)
    pre_other = send(pick(pre_split, 1 - c, 1), cores)
    out_grad2 = jnp.concatenate([out_grad, send(out_grad, cores)], 0)
    inputs2 = jnp.concatenate([inputs, send(inputs, cores)], 0)
    pre2 = jnp.concatenate([pre_mine, pre_other], 0)

    parts = [[send(w_out, gather_perm(i, j)) for j in range(nl)] for i in range(2)]
    parts = jnp.stack([jnp.stack(p, 0) for p in parts], 0)
    by_z = jnp.stack(
        [
            jnp.stack([parts[cc ^ high, ll ^ low] for cc in range(2)], 0)
            for ll in range(nl)
        ],
        0,
    )

    def gather_plane(array, cut):
        one, two = jnp.split(array, 2, cut)
        one = paired(one, send(one, along_x), x, 0)
        two = paired(two, send(two, along_y), y, 0)
        one = paired(one, send(one, along_y), y, 0)
        two = paired(two, send(two, along_x), x, 1)
        return jnp.concatenate([one, two], cut + 2)

    w_out2 = gather_plane(by_z, 1).transpose(2, 0, 1, 3, 4, 5).reshape(half, width)

    in_split = w_in.reshape(rows_in, 2, half)
    in_two = paired(pick(in_split, c, 1), send(pick(in_split, 1 - c, 1), cores), c, 0)
    parts = jnp.stack([in_two] + [send(in_two, z_perm(k)) for k in range(1, nz)], 0)
    by_z = jnp.stack([parts[zz ^ z] for zz in range(nz)], 0)
    w_in2 = gather_plane(by_z, 3).transpose(2, 0, 1, 3, 4, 5).reshape(width, half)

    def scatter_plane(total, cut):
        one, two = jnp.split(total, 2, cut)
        one = pick(one, x, 2) + send(pick(one, 1 - x, 2).astype(BF), along_x).astype(F32)
        two = pick(two, y, 1) + send(pick(two, 1 - y, 1).astype(BF), along_y).astype(F32)
        one = pick(one, y, 1) + send(pick(one, 1 - y, 1).astype(BF), along_y).astype(F32)
        two = pick(two, x, 1) + send(pick(two, 1 - x, 1).astype(BF), along_x).astype(F32)
        return jnp.concatenate([one, two], cut - 2)

    activ, slope = gelu_parts(pre2)
    total = contract_first(activ, out_grad2)
    total = total.reshape(nl, 2, 2, 2, rows_out, width)
    total = scatter_plane(total, 3)
    narrow = total.astype(BF)
    w_out_grad = 0.0
    for i in range(2):
        for j in range(nl):
            sent = send(narrow[low ^ j, high ^ i], scatter_perm(i, j)).astype(F32)
            if i == 0 and j == 0:
                sent = jnp.where(c == high, total[low, high], sent)
            w_out_grad = w_out_grad + sent
    w_out_grad = w_out_grad * grad_scale

    act_grad = contract_last(out_grad2, w_out2)
    pre_grad = (act_grad * slope).astype(BF)

    total = contract_first(inputs2, pre_grad)
    total = total.reshape(nz, 2, 2, 2 * rows_in, half)
    total = scatter_plane(total, 4)
    narrow = total.astype(BF)
    own = total[z]
    for k in range(1, nz):
        own = own + send(narrow[z ^ k], z_perm(k)).astype(F32)
    own = (own * grad_scale).reshape(2, rows_in, half)
    w_in_grad = paired(own[c], send(own[1 - c], cores), c, 1).reshape(rows_in, hidden)

    part = contract_last(pre_grad, w_in2)
    input_grad = part[:tokens] + send(part[tokens:], cores)
    return (input_grad, w_out_grad, w_in_grad)


MIB = 1 << 20
ANY = pl.BlockSpec(memory_space=pl.ANY)
VMEM = pl.BlockSpec(memory_space=pltpu.VMEM)
SMEM = pl.BlockSpec(memory_space=pltpu.SMEM)


def shape(dims, kind):
    return jax.ShapeDtypeStruct(dims, kind)


class Order:
    def __init__(self):
        self.after = []

    def __call__(self, outs):
        self.after = [outs[0]]
        return outs


def small(body, where, arrays, outs, after=(), scratch=(), name=None, flops=0):
    skipped = len(after)

    def run(*refs):
        body(*refs[: 1 + len(arrays)], *refs[1 + len(arrays) + skipped :])

    moved_bytes = sum(a.size * a.dtype.itemsize for a in list(arrays) + list(outs))
    return pl.pallas_call(
        run,
        name=name or body.__name__,
        out_shape=outs,
        in_specs=[SMEM] + [VMEM] * len(arrays) + [ANY] * skipped,
        out_specs=[VMEM] * len(outs),
        scratch_shapes=list(scratch),
        compiler_params=pltpu.CompilerParams(vmem_limit_bytes=16 * MIB),
        cost_estimate=pl.CostEstimate(
            flops=flops, bytes_accessed=moved_bytes, transcendentals=0
        ),
    )(where, *arrays, *after)


def pair_kernel(at, in_ref, got_ref, out):
    c = at[3]
    size = out.shape[2]
    out[c] = jnp.where(c == 0, in_ref[:, :size], in_ref[:, size:])
    out[1 - c] = jnp.where(c == 0, got_ref[:, :size], got_ref[:, size:])


def join_kernel(at, own1, got1, own2, got2, one, two):
    x, y = at[2], at[1]
    one[x] = own1[...]
    one[1 - x] = got1[...]
    two[y] = own2[...]
    two[1 - y] = got2[...]


def rows_kernel(at, g00, g01, g10, g11, one, two):
    high, low = at[4], at[5]
    rows = g00.shape[0]
    for cc in range(2):
        from_same = jnp.where(high == cc, g00[...], g10[...])
        from_next = jnp.where(high == cc, g01[...], g11[...])
        part = pl.ds(cc * rows, rows)
        one[part, :] = jnp.where(low == 0, from_same, from_next)
        two[part, :] = jnp.where(low == 0, from_next, from_same)


def columns_kernel(at, mine, g1, g2, g3, one, two):
    z = at[0]
    rows, size = mine.shape[0] * mine.shape[1], one.shape[2]
    for k, got in enumerate((mine, g1, g2, g3)):
        value = got[...].reshape(rows, 2 * size)
        one[z ^ k] = value[:, :size]
        two[z ^ k] = value[:, size:]


def out_total(at, cut, pre, pre_got, grad, grad_got, after):
    tokens, width = grad.shape
    size = pre_got.shape[1] // 8
    rows = size // 2

    def body(at, pre_ref, got_ref, grad_ref, grad2_ref, *refs):
        slope, send, keep, total = refs[-4:]
        t = pl.program_id(0)
        x, y = at[2], at[1]
        activ, slope1 = gelu_parts(pre_ref[...])
        slope[pl.ds(0, tokens), :] = slope1
        value = contract_first(activ, grad_ref[...])
        activ, slope2 = gelu_parts(got_ref[...])
        slope[pl.ds(tokens, tokens), :] = slope2
        value = value + contract_first(activ, grad2_ref[...])
        if cut == 0:
            total[...] = value.reshape(2, rows, width)
            send[0] = total[1 - x].astype(BF)
            keep[0] = total[x]
        else:

            @pl.when(t == y)
            def _():
                keep[...] = value.reshape(2, rows, width)

            @pl.when(t != y)
            def _():
                send[...] = value.astype(BF).reshape(2, rows, width)

    whole = lambda t, at: (0, 0)
    if cut == 0:
        parts = pl.BlockSpec((1, rows, width), lambda t, at: (t, 0, 0))
    else:
        parts = pl.BlockSpec((2, rows, width), lambda t, at: (0, 0, 0))
    return pl.pallas_call(
        body,
        name=f"out_total{cut}",
        grid_spec=pltpu.PrefetchScalarGridSpec(
            num_scalar_prefetch=1,
            grid=(2,),
            in_specs=[
                pl.BlockSpec((tokens, size), lambda t, at: (0, at[3] * 4 + cut * 2 + t)),
                pl.BlockSpec((tokens, size), lambda t, at: (0, at[3] * 4 + cut * 2 + t)),
                pl.BlockSpec((tokens, width), whole),
                pl.BlockSpec((tokens, width), whole),
            ]
            + [ANY] * len(after),
            out_specs=[
                pl.BlockSpec((2 * tokens, size), lambda t, at: (0, t)),
                parts,
                parts,
            ],
            scratch_shapes=[pltpu.VMEM((2, rows, width), F32)],
        ),
        out_shape=[
            shape((2 * tokens, 2 * size), F32),
            shape((2, rows, width), BF),
            shape((2, rows, width), F32),
        ],
        compiler_params=pltpu.CompilerParams(vmem_limit_bytes=24 * MIB),
        cost_estimate=pl.CostEstimate(
            flops=8 * tokens * size * width,
            bytes_accessed=20 * MIB,
            transcendentals=4 * tokens * size,
        ),
    )(at, pre, pre_got, grad, grad_got, *after)


def in_total(at, cut, grad, grad_got, inputs, inputs_got, slope, pieces, nz, after):
    tokens, width = grad.shape
    size = slope.shape[1] // 2
    rows = size // 2
    depth = width // (4 * nz)

    def body(at, grad_ref, grad2_ref, in_ref, in2_ref, slope_ref, mine, other, _, pre_grad, send, keep):
        t = pl.program_id(0)
        x, y = at[2], at[1]
        if cut == 0:
            value = jnp.where(t == y, mine[...], other[...]).reshape(size, width)
        else:
            first, second = mine[t], other[t]
            value = jnp.concatenate(
                [jnp.where(x == 0, first, second), jnp.where(x == 0, second, first)], 0
            )
        totals = 0.0
        for part, (g, i) in enumerate(((grad_ref, in_ref), (grad2_ref, in2_ref))):
            at_rows = pl.ds(part * tokens, tokens)
            act_grad = contract_last(g[...], value)
            pre = (act_grad * slope_ref[at_rows, :]).astype(BF)
            pre_grad[at_rows, :] = pre
            totals = totals + contract_first(i[...], pre)
        parts = totals.reshape(nz, 2, 2, depth, size)
        if cut == 0:
            first, second, bit = parts[:, :, 0], parts[:, :, 1], x
        else:
            first, second, bit = parts[:, 0], parts[:, 1], y
        send[...] = jnp.where(bit == 0, second, first).astype(BF)
        keep[...] = jnp.where(bit == 0, first, second)

    whole = lambda t, at: (0, 0)
    tile = lambda t, at: (0, t)
    piece = pl.BlockSpec((2, rows, width), lambda t, at: (0, 0, 0))
    parts = pl.BlockSpec((nz, 2, depth, size), lambda t, at: (0, 0, 0, t))
    return pl.pallas_call(
        body,
        name=f"in_total{cut}",
        grid_spec=pltpu.PrefetchScalarGridSpec(
            num_scalar_prefetch=1,
            grid=(2,),
            in_specs=[pl.BlockSpec((tokens, width), whole)] * 4
            + [pl.BlockSpec((2 * tokens, size), tile)]
            + [piece] * 2
            + [ANY],
            out_specs=[pl.BlockSpec((2 * tokens, size), tile), parts, parts],
        ),
        out_shape=[
            shape((2 * tokens, 2 * size), BF),
            shape((nz, 2, depth, 2 * size), BF),
            shape((nz, 2, depth, 2 * size), F32),
        ],
        compiler_params=pltpu.CompilerParams(vmem_limit_bytes=24 * MIB),
        cost_estimate=pl.CostEstimate(
            flops=16 * tokens * size * width, bytes_accessed=16 * MIB, transcendentals=0
        ),
    )(at, grad, grad_got, inputs, inputs_got, slope, *pieces, *after)


def input_part(at, pre_grads, pieces, nz, after):
    tokens, size = pre_grads[0].shape[0] // 2, pre_grads[0].shape[1]
    depth = pieces[0].shape[2]
    width = 4 * nz * depth

    def body(at, g0, g1, a0, a1, b0, b1, _, mine, other, weight0, weight1):
        t = pl.program_id(0)
        x, y = at[2], at[1]

        @pl.when(t == 0)
        def _():
            for k in range(2):
                weight0[:, y, k] = a0[k]
                weight0[:, 1 - y, k] = a1[k]
                weight1[:, k, x] = b0[k]
                weight1[:, k, 1 - x] = b1[k]

        value = contract_last(g0[...], weight0[...].reshape(width, size))
        value = value + contract_last(g1[...], weight1[...].reshape(width, size))

        @pl.when(t == 0)
        def _():
            other[...] = value

        @pl.when(t == 1)
        def _():
            mine[...] = value

    piece = pl.BlockSpec((2, nz, depth, size), lambda t, at: (0, 0, 0, 0))
    rows = pl.BlockSpec((tokens, size), lambda t, at: (1 - t, 0))
    out = pl.BlockSpec((tokens, width), lambda t, at: (0, 0))
    return pl.pallas_call(
        body,
        name="input_part",
        grid_spec=pltpu.PrefetchScalarGridSpec(
            num_scalar_prefetch=1,
            grid=(2,),
            in_specs=[rows] * 2 + [piece] * 4 + [ANY],
            out_specs=[out, out],
            scratch_shapes=[pltpu.VMEM((nz, 2, 2, depth, size), BF)] * 2,
        ),
        out_shape=[shape((tokens, width), F32)] * 2,
        compiler_params=pltpu.CompilerParams(vmem_limit_bytes=24 * MIB),
        cost_estimate=pl.CostEstimate(
            flops=8 * tokens * size * width, bytes_accessed=10 * MIB, transcendentals=0
        ),
    )(at, *pre_grads, *pieces, *after)


def per_device(out_grad, inputs, preact, w_out, w_in):
    n = lax.axis_size(AXIS)
    rows_out, rows_in = w_out.shape[0], w_in.shape[0]
    if n != 32 or rows_out % 16 or (2 * rows_in) % 16 or out_grad.shape[1] % 128:
        return plain(out_grad, inputs, preact, w_out, w_in)
    nz = n // 8
    nl = nz // 2
    me = lax.axis_index(AXIS)
    z, y, x, c = coords(me)
    at = jnp.stack([z, y, x, c, z // nl, z % nl]).astype(jnp.int32)
    grad_scale = 1.0 / math.sqrt(out_grad.shape[0] * n)
    tokens, width = out_grad.shape
    hidden = preact.shape[1]
    half = hidden // 2
    size = half // 2

    along_x = moved(n, lambda z, y, x, c: (z, y, 1 - x, c))
    along_y = moved(n, lambda z, y, x, c: (z, 1 - y, x, c))

    def send(array, perm):
        return lax.ppermute(array, AXIS, perm)

    def z_perm(k, swap=0):
        return moved(n, lambda z, y, x, c: (z ^ k, y, x, c ^ swap))

    def gather_perm(i, j):
        return moved(
            n, lambda z, y, x, c: ((c ^ i) * nl + ((z % nl) ^ j), y, x, z // nl)
        )

    def scatter_perm(i, j):
        return moved(
            n, lambda z, y, x, c: (c * nl + ((z % nl) ^ j), y, x, (z // nl) ^ i)
        )

    order = Order()

    def kernel(body, arrays, outs, scratch=(), name=None, flops=0):
        return order(small(body, at, arrays, outs, order.after, scratch, name, flops))

    pre_got = send(preact, z_perm(0, 1))
    grad_got = send(out_grad, z_perm(0, 1))
    got = [send(w_out, gather_perm(i, j)) for i in range(2) for j in range(2)]
    inputs_got = send(inputs, z_perm(0, 1))
    in_got = send(w_in, z_perm(0, 1))

    slopes, sent, kept = [None] * 2, [None] * 2, [None] * 2

    def out_cut(cut):
        s, o, k = out_total(at, cut, preact, pre_got, out_grad, grad_got, order.after)
        order([o])
        slopes[cut], kept[cut] = s, k
        sent[cut] = send(o, (along_x, along_y)[cut])

    def middle(k, r, next_perm, bit, dim):
        dims = k.shape[:dim] + k.shape[dim + 1 :]

        def body(at, k_ref, r_ref, out, keep):
            b = at[bit]
            spot = (slice(None),) * dim
            out[...] = (k_ref[spot + (1 - b,)] + r_ref[spot + (1 - b,)].astype(F32)).astype(BF)
            keep[...] = k_ref[spot + (b,)] + r_ref[spot + (b,)].astype(F32)

        out, keep = kernel(body, [k, r], [shape(dims, BF), shape(dims, F32)], name=f"middle{dim}{bit}")
        return keep, send(out, next_perm)

    def join(one, one_got, two, two_got):
        pair = shape((2,) + one.shape, BF)
        return kernel(join_kernel, [one, one_got, two, two_got], [pair, pair])

    order.after = [inputs_got]
    out_cut(0)

    (in_two,) = kernel(pair_kernel, [w_in, in_got], [shape((2, rows_in, half), BF)])
    in_z = [send(in_two, z_perm(k)) for k in range(1, nz)]

    rows = shape((2 * rows_out, width), BF)
    one, two = kernel(rows_kernel, got, [rows, rows])
    one_got, two_got = send(one, along_x), send(two, along_y)
    out_cut(1)
    ones, twos = join(one, one_got, two, two_got)
    ones_got, twos_got = send(ones, along_y), send(twos, along_x)

    out_sides = [middle(kept[0], sent[0], along_y, 1, 0), middle(kept[1], sent[1], along_x, 2, 0)]

    spread = shape((nz, 2 * rows_in, size), BF)
    one, two = kernel(columns_kernel, [in_two] + in_z, [spread, spread])
    in_pieces = [one, send(one, along_x), two, send(two, along_y)]

    pre_grads, in_sent, in_kept = [None] * 2, [None] * 2, [None] * 2

    def in_cut(cut, pieces):
        p, o, k = in_total(
            at, cut, out_grad, grad_got, inputs, inputs_got, slopes[cut], pieces, nz, order.after
        )
        order([o])
        pre_grads[cut], in_kept[cut] = p, k
        in_sent[cut] = send(o, (along_x, along_y)[cut])

    in_cut(0, [ones, ones_got])

    def out_parts(at, k1, r1, k2, r2, o00, o01, o10, o11, own, total):
        high, low = at[4], at[5]
        total[0] = (k1[...] + r1[...].astype(F32)).reshape(2, rows_out, width)
        total[1] = (k2[...] + r2[...].astype(F32)).reshape(2, rows_out, width)
        own[...] = total[low, high]
        o00[...] = total[low, high].astype(BF)
        o01[...] = total[1 - low, high].astype(BF)
        o10[...] = total[low, 1 - high].astype(BF)
        o11[...] = total[1 - low, 1 - high].astype(BF)

    row = (rows_out, width)
    *out_got, out_own = kernel(
        out_parts,
        [*out_sides[0], *out_sides[1]],
        [shape(row, BF)] * 4 + [shape(row, F32)],
        [pltpu.VMEM((2, 2, rows_out, width), F32)],
    )
    out_got = [send(p, scatter_perm(*divmod(k, 2))) for k, p in enumerate(out_got)]

    in_cut(1, [twos, twos_got])

    def out_sum(at, own, r00, r01, r10, r11, out):
        first = jnp.where(at[3] == at[4], own[...], r00[...].astype(F32))
        rest = r01[...].astype(F32) + r10[...].astype(F32) + r11[...].astype(F32)
        out[...] = (first + rest) * grad_scale

    (w_out_grad,) = kernel(out_sum, [out_own] + out_got, [shape(out_own.shape, F32)])

    order.after = order.after + [in_pieces[1], in_pieces[3]]
    one, one_got = middle(in_kept[0], in_sent[0], along_y, 1, 1)
    two, two_got = middle(in_kept[1], in_sent[1], along_x, 2, 1)

    def in_parts(at, k1, r1, k2, r2, *outs):
        z = at[0]
        *outs, own, total = outs
        total[:, :, :size] = k1[...] + r1[...].astype(F32)
        total[:, :, size:] = k2[...] + r2[...].astype(F32)
        own[...] = total[z]
        for k in range(1, nz):
            outs[k - 1][...] = total[z ^ k].astype(BF)

    row = (2 * rows_in, half)
    *in_got, in_own = kernel(
        in_parts,
        [one, one_got, two, two_got],
        [shape(row, BF)] * (nz - 1) + [shape(row, F32)],
        [pltpu.VMEM((nz, 2 * rows_in, half), F32)],
    )
    in_got = [send(p, z_perm(k)) for p, k in zip(in_got, range(1, nz))]

    ones, twos = join(*in_pieces)
    in_pieces = [ones, send(ones, along_y), twos, send(twos, along_x)]

    part, part_other = input_part(at, pre_grads, in_pieces, nz, order.after)
    order([part_other])
    part_got = send(part_other, z_perm(0, 1))

    def in_sum(at, own, r1, r2, r3, mine, other):
        total = own[...] + r1[...].astype(F32) + r2[...].astype(F32) + r3[...].astype(F32)
        total = total * grad_scale
        first, second = total[:rows_in], total[rows_in:]
        mine[...] = jnp.where(at[3] == 0, first, second)
        other[...] = jnp.where(at[3] == 0, second, first)

    row = shape((rows_in, half), F32)
    mine, other = kernel(in_sum, [in_own] + in_got, [row, row], flops=10**11)
    other = send(other, z_perm(0, 1))

    def input_sum(at, mine, other, out):
        out[...] = mine[...] + other[...]

    (input_grad,) = kernel(input_sum, [part, part_got], [shape((tokens, width), F32)])

    return (input_grad, w_out_grad, w_in_grad)


MIB = 1 << 20
ANY = pl.BlockSpec(memory_space=pl.ANY)
VMEM = pl.BlockSpec(memory_space=pltpu.VMEM)
SMEM = pl.BlockSpec(memory_space=pltpu.SMEM)


def shape(dims, kind):
    return jax.ShapeDtypeStruct(dims, kind)


class Order:
    def __init__(self):
        self.after = []

    def __call__(self, outs):
        self.after = [outs[0]]
        return outs


def small(body, where, arrays, outs, after=(), scratch=(), name=None, flops=0):
    skipped = len(after)

    def run(*refs):
        body(*refs[: 1 + len(arrays)], *refs[1 + len(arrays) + skipped :])

    moved_bytes = sum(a.size * a.dtype.itemsize for a in list(arrays) + list(outs))
    return pl.pallas_call(
        run,
        name=name or body.__name__,
        out_shape=outs,
        in_specs=[SMEM] + [VMEM] * len(arrays) + [ANY] * skipped,
        out_specs=[VMEM] * len(outs),
        scratch_shapes=list(scratch),
        compiler_params=pltpu.CompilerParams(vmem_limit_bytes=16 * MIB),
        cost_estimate=pl.CostEstimate(
            flops=flops, bytes_accessed=moved_bytes, transcendentals=0
        ),
    )(where, *arrays, *after)


def pair_kernel(at, in_ref, got_ref, out):
    c = at[3]
    size = out.shape[2]
    out[c] = jnp.where(c == 0, in_ref[:, :size], in_ref[:, size:])
    out[1 - c] = jnp.where(c == 0, got_ref[:, :size], got_ref[:, size:])


def join_kernel(at, own1, got1, own2, got2, one, two):
    x, y = at[2], at[1]
    one[x] = own1[...]
    one[1 - x] = got1[...]
    two[y] = own2[...]
    two[1 - y] = got2[...]


def rows_kernel(at, g00, g01, g10, g11, one, two):
    high, low = at[4], at[5]
    rows = g00.shape[0]
    for cc in range(2):
        from_same = jnp.where(high == cc, g00[...], g10[...])
        from_next = jnp.where(high == cc, g01[...], g11[...])
        part = pl.ds(cc * rows, rows)
        one[part, :] = jnp.where(low == 0, from_same, from_next)
        two[part, :] = jnp.where(low == 0, from_next, from_same)


def columns_kernel(at, mine, g1, g2, g3, one, two):
    z = at[0]
    rows, size = mine.shape[0] * mine.shape[1], one.shape[2]
    for k, got in enumerate((mine, g1, g2, g3)):
        value = got[...].reshape(rows, 2 * size)
        one[z ^ k] = value[:, :size]
        two[z ^ k] = value[:, size:]


def out_total(at, cut, pre, pre_got, grad, grad_got, after):
    tokens, width = grad.shape
    size = pre_got.shape[1] // 8
    rows = size // 2

    def body(at, pre_ref, got_ref, grad_ref, grad2_ref, *refs):
        slope, send, keep, total = refs[-4:]
        t = pl.program_id(0)
        x, y = at[2], at[1]
        activ, slope1 = gelu_parts(pre_ref[...])
        slope[pl.ds(0, tokens), :] = slope1
        value = contract_first(activ, grad_ref[...])
        activ, slope2 = gelu_parts(got_ref[...])
        slope[pl.ds(tokens, tokens), :] = slope2
        value = value + contract_first(activ, grad2_ref[...])
        if cut == 0:
            total[...] = value.reshape(2, rows, width)
            send[0] = total[1 - x].astype(BF)
            keep[0] = total[x]
        else:

            @pl.when(t == y)
            def _():
                keep[...] = value.reshape(2, rows, width)

            @pl.when(t != y)
            def _():
                send[...] = value.astype(BF).reshape(2, rows, width)

    whole = lambda t, at: (0, 0)
    if cut == 0:
        parts = pl.BlockSpec((1, rows, width), lambda t, at: (t, 0, 0))
    else:
        parts = pl.BlockSpec((2, rows, width), lambda t, at: (0, 0, 0))
    return pl.pallas_call(
        body,
        name=f"out_total{cut}",
        grid_spec=pltpu.PrefetchScalarGridSpec(
            num_scalar_prefetch=1,
            grid=(2,),
            in_specs=[
                pl.BlockSpec((tokens, size), lambda t, at: (0, at[3] * 4 + cut * 2 + t)),
                pl.BlockSpec((tokens, size), lambda t, at: (0, at[3] * 4 + cut * 2 + t)),
                pl.BlockSpec((tokens, width), whole),
                pl.BlockSpec((tokens, width), whole),
            ]
            + [ANY] * len(after),
            out_specs=[
                pl.BlockSpec((2 * tokens, size), lambda t, at: (0, t)),
                parts,
                parts,
            ],
            scratch_shapes=[pltpu.VMEM((2, rows, width), F32)],
        ),
        out_shape=[
            shape((2 * tokens, 2 * size), F32),
            shape((2, rows, width), BF),
            shape((2, rows, width), F32),
        ],
        compiler_params=pltpu.CompilerParams(vmem_limit_bytes=24 * MIB),
        cost_estimate=pl.CostEstimate(
            flops=8 * tokens * size * width,
            bytes_accessed=20 * MIB,
            transcendentals=4 * tokens * size,
        ),
    )(at, pre, pre_got, grad, grad_got, *after)


def in_total(at, cut, grad, grad_got, inputs, inputs_got, slope, pieces, nz, after):
    tokens, width = grad.shape
    size = slope.shape[1] // 2
    rows = size // 2
    depth = width // (4 * nz)

    def body(at, grad_ref, grad2_ref, in_ref, in2_ref, slope_ref, mine, other, _, pre_grad, send, keep):
        t = pl.program_id(0)
        x, y = at[2], at[1]
        if cut == 0:
            value = jnp.where(t == y, mine[...], other[...]).reshape(size, width)
        else:
            first, second = mine[t], other[t]
            value = jnp.concatenate(
                [jnp.where(x == 0, first, second), jnp.where(x == 0, second, first)], 0
            )
        totals = 0.0
        for part, (g, i) in enumerate(((grad_ref, in_ref), (grad2_ref, in2_ref))):
            at_rows = pl.ds(part * tokens, tokens)
            act_grad = contract_last(g[...], value)
            pre = (act_grad * slope_ref[at_rows, :]).astype(BF)
            pre_grad[at_rows, :] = pre
            totals = totals + contract_first(i[...], pre)
        parts = totals.reshape(nz, 2, 2, depth, size)
        if cut == 0:
            first, second, bit = parts[:, :, 0], parts[:, :, 1], x
        else:
            first, second, bit = parts[:, 0], parts[:, 1], y
        send[...] = jnp.where(bit == 0, second, first).astype(BF)
        keep[...] = jnp.where(bit == 0, first, second)

    whole = lambda t, at: (0, 0)
    tile = lambda t, at: (0, t)
    piece = pl.BlockSpec((2, rows, width), lambda t, at: (0, 0, 0))
    parts = pl.BlockSpec((nz, 2, depth, size), lambda t, at: (0, 0, 0, t))
    return pl.pallas_call(
        body,
        name=f"in_total{cut}",
        grid_spec=pltpu.PrefetchScalarGridSpec(
            num_scalar_prefetch=1,
            grid=(2,),
            in_specs=[pl.BlockSpec((tokens, width), whole)] * 4
            + [pl.BlockSpec((2 * tokens, size), tile)]
            + [piece] * 2
            + [ANY],
            out_specs=[pl.BlockSpec((2 * tokens, size), tile), parts, parts],
        ),
        out_shape=[
            shape((2 * tokens, 2 * size), BF),
            shape((nz, 2, depth, 2 * size), BF),
            shape((nz, 2, depth, 2 * size), F32),
        ],
        compiler_params=pltpu.CompilerParams(vmem_limit_bytes=24 * MIB),
        cost_estimate=pl.CostEstimate(
            flops=16 * tokens * size * width, bytes_accessed=16 * MIB, transcendentals=0
        ),
    )(at, grad, grad_got, inputs, inputs_got, slope, *pieces, *after)


def input_part(at, pre_grads, pieces, nz, after):
    tokens, size = pre_grads[0].shape[0] // 2, pre_grads[0].shape[1]
    depth = pieces[0].shape[2]
    width = 4 * nz * depth

    def body(at, g0, g1, a0, a1, b0, b1, _, mine, other, weight0, weight1):
        t = pl.program_id(0)
        x, y = at[2], at[1]

        @pl.when(t == 0)
        def _():
            for k in range(2):
                weight0[:, y, k] = a0[k]
                weight0[:, 1 - y, k] = a1[k]
                weight1[:, k, x] = b0[k]
                weight1[:, k, 1 - x] = b1[k]

        value = contract_last(g0[...], weight0[...].reshape(width, size))
        value = value + contract_last(g1[...], weight1[...].reshape(width, size))

        @pl.when(t == 0)
        def _():
            other[...] = value

        @pl.when(t == 1)
        def _():
            mine[...] = value

    piece = pl.BlockSpec((2, nz, depth, size), lambda t, at: (0, 0, 0, 0))
    rows = pl.BlockSpec((tokens, size), lambda t, at: (1 - t, 0))
    out = pl.BlockSpec((tokens, width), lambda t, at: (0, 0))
    return pl.pallas_call(
        body,
        name="input_part",
        grid_spec=pltpu.PrefetchScalarGridSpec(
            num_scalar_prefetch=1,
            grid=(2,),
            in_specs=[rows] * 2 + [piece] * 4 + [ANY],
            out_specs=[out, out],
            scratch_shapes=[pltpu.VMEM((nz, 2, 2, depth, size), BF)] * 2,
        ),
        out_shape=[shape((tokens, width), F32)] * 2,
        compiler_params=pltpu.CompilerParams(vmem_limit_bytes=24 * MIB),
        cost_estimate=pl.CostEstimate(
            flops=8 * tokens * size * width, bytes_accessed=10 * MIB, transcendentals=0
        ),
    )(at, *pre_grads, *pieces, *after)


def per_device(out_grad, inputs, preact, w_out, w_in):
    n = lax.axis_size(AXIS)
    rows_out, rows_in = w_out.shape[0], w_in.shape[0]
    if n != 32 or rows_out % 16 or (2 * rows_in) % 16 or out_grad.shape[1] % 128:
        return plain(out_grad, inputs, preact, w_out, w_in)
    nz = n // 8
    nl = nz // 2
    me = lax.axis_index(AXIS)
    z, y, x, c = coords(me)
    at = jnp.stack([z, y, x, c, z // nl, z % nl]).astype(jnp.int32)
    grad_scale = 1.0 / math.sqrt(out_grad.shape[0] * n)
    tokens, width = out_grad.shape
    hidden = preact.shape[1]
    half = hidden // 2
    size = half // 2

    along_x = moved(n, lambda z, y, x, c: (z, y, 1 - x, c))
    along_y = moved(n, lambda z, y, x, c: (z, 1 - y, x, c))

    def send(array, perm):
        return lax.ppermute(array, AXIS, perm)

    def z_perm(k, swap=0):
        return moved(n, lambda z, y, x, c: (z ^ k, y, x, c ^ swap))

    def gather_perm(i, j):
        return moved(
            n, lambda z, y, x, c: ((c ^ i) * nl + ((z % nl) ^ j), y, x, z // nl)
        )

    def scatter_perm(i, j):
        return moved(
            n, lambda z, y, x, c: (c * nl + ((z % nl) ^ j), y, x, (z // nl) ^ i)
        )

    order = Order()

    def kernel(body, arrays, outs, scratch=(), name=None, flops=0):
        return order(small(body, at, arrays, outs, order.after, scratch, name, flops))

    pre_got = send(preact, z_perm(0, 1))
    grad_got = send(out_grad, z_perm(0, 1))
    got = [send(w_out, gather_perm(i, j)) for i in range(2) for j in range(2)]
    inputs_got = send(inputs, z_perm(0, 1))
    in_got = send(w_in, z_perm(0, 1))

    slopes, sent, kept = [None] * 2, [None] * 2, [None] * 2

    def out_cut(cut):
        s, o, k = out_total(at, cut, preact, pre_got, out_grad, grad_got, order.after)
        order([o])
        slopes[cut], kept[cut] = s, k
        sent[cut] = send(o, (along_x, along_y)[cut])

    def middle(k, r, next_perm, bit, dim):
        dims = k.shape[:dim] + k.shape[dim + 1 :]

        def body(at, k_ref, r_ref, out, keep):
            b = at[bit]
            spot = (slice(None),) * dim
            out[...] = (k_ref[spot + (1 - b,)] + r_ref[spot + (1 - b,)].astype(F32)).astype(BF)
            keep[...] = k_ref[spot + (b,)] + r_ref[spot + (b,)].astype(F32)

        out, keep = kernel(body, [k, r], [shape(dims, BF), shape(dims, F32)], name=f"middle{dim}{bit}")
        return keep, send(out, next_perm)

    def join(one, one_got, two, two_got):
        pair = shape((2,) + one.shape, BF)
        return kernel(join_kernel, [one, one_got, two, two_got], [pair, pair])

    order.after = [inputs_got]
    out_cut(0)

    (in_two,) = kernel(pair_kernel, [w_in, in_got], [shape((2, rows_in, half), BF)])
    in_z = [send(in_two, z_perm(k)) for k in range(1, nz)]

    rows = shape((2 * rows_out, width), BF)
    one, two = kernel(rows_kernel, got, [rows, rows])
    one_got, two_got = send(one, along_x), send(two, along_y)
    out_cut(1)
    ones, twos = join(one, one_got, two, two_got)
    ones_got, twos_got = send(ones, along_y), send(twos, along_x)

    out_sides = [middle(kept[0], sent[0], along_y, 1, 0), middle(kept[1], sent[1], along_x, 2, 0)]

    spread = shape((nz, 2 * rows_in, size), BF)
    one, two = kernel(columns_kernel, [in_two] + in_z, [spread, spread])
    in_pieces = [one, send(one, along_x), two, send(two, along_y)]

    pre_grads, in_sent, in_kept = [None] * 2, [None] * 2, [None] * 2

    def in_cut(cut, pieces):
        p, o, k = in_total(
            at, cut, out_grad, grad_got, inputs, inputs_got, slopes[cut], pieces, nz, order.after
        )
        order([o])
        pre_grads[cut], in_kept[cut] = p, k
        in_sent[cut] = send(o, (along_x, along_y)[cut])

    in_cut(0, [ones, ones_got])

    def out_parts(at, k1, r1, k2, r2, o00, o01, o10, o11, own, total):
        high, low = at[4], at[5]
        total[0] = (k1[...] + r1[...].astype(F32)).reshape(2, rows_out, width)
        total[1] = (k2[...] + r2[...].astype(F32)).reshape(2, rows_out, width)
        own[...] = total[low, high]
        o00[...] = total[low, high].astype(BF)
        o01[...] = total[1 - low, high].astype(BF)
        o10[...] = total[low, 1 - high].astype(BF)
        o11[...] = total[1 - low, 1 - high].astype(BF)

    row = (rows_out, width)
    *out_got, out_own = kernel(
        out_parts,
        [*out_sides[0], *out_sides[1]],
        [shape(row, BF)] * 4 + [shape(row, F32)],
        [pltpu.VMEM((2, 2, rows_out, width), F32)],
    )
    out_got = [send(p, scatter_perm(*divmod(k, 2))) for k, p in enumerate(out_got)]

    in_cut(1, [twos, twos_got])

    def out_sum(at, own, r00, r01, r10, r11, out):
        first = jnp.where(at[3] == at[4], own[...], r00[...].astype(F32))
        rest = r01[...].astype(F32) + r10[...].astype(F32) + r11[...].astype(F32)
        out[...] = (first + rest) * grad_scale

    (w_out_grad,) = kernel(out_sum, [out_own] + out_got, [shape(out_own.shape, F32)])

    order.after = order.after + [in_pieces[1], in_pieces[3]]
    one, one_got = middle(in_kept[0], in_sent[0], along_y, 1, 1)
    two, two_got = middle(in_kept[1], in_sent[1], along_x, 2, 1)

    def in_parts(at, k1, r1, k2, r2, *outs):
        z = at[0]
        *outs, own, total = outs
        total[:, :, :size] = k1[...] + r1[...].astype(F32)
        total[:, :, size:] = k2[...] + r2[...].astype(F32)
        own[...] = total[z]
        for k in range(1, nz):
            outs[k - 1][...] = total[z ^ k].astype(BF)

    row = (2 * rows_in, half)
    *in_got, in_own = kernel(
        in_parts,
        [one, one_got, two, two_got],
        [shape(row, BF)] * (nz - 1) + [shape(row, F32)],
        [pltpu.VMEM((nz, 2 * rows_in, half), F32)],
    )
    in_got = [send(p, z_perm(k)) for p, k in zip(in_got, range(1, nz))]

    ones, twos = join(*in_pieces)
    in_pieces = [ones, send(ones, along_y), twos, send(twos, along_x)]

    part, part_other = input_part(at, pre_grads, in_pieces, nz, order.after)
    order([part_other])
    part_got = send(part_other, z_perm(0, 1))

    def in_sum(at, own, r1, r2, r3, mine, other):
        total = own[...] + r1[...].astype(F32) + r2[...].astype(F32) + r3[...].astype(F32)
        total = total * grad_scale
        first, second = total[:rows_in], total[rows_in:]
        mine[...] = jnp.where(at[3] == 0, first, second)
        other[...] = jnp.where(at[3] == 0, second, first)

    row = shape((rows_in, half), F32)
    mine, other = kernel(in_sum, [in_own] + in_got, [row, row], flops=10**11)
    other = send(other, z_perm(0, 1))

    def input_sum(at, mine, other, out):
        out[...] = mine[...] + other[...]

    (input_grad,) = kernel(input_sum, [part, part_got], [shape((tokens, width), F32)])

    def in_join(at, mine, other, out):
        c = at[3]
        out[:, :half] = jnp.where(c == 0, mine[...], other[...])
        out[:, half:] = jnp.where(c == 0, other[...], mine[...])

    (w_in_grad,) = kernel(in_join, [mine, other], [shape((rows_in, hidden), F32)])
    return (input_grad, w_out_grad, w_in_grad)


def solution(mesh):
    in_specs = (
        P(("grp", "gx"), None),
        P(("grp", "gx"), None),
        P(("grp", "gx"), None),
        P("gx", None),
        P("gx", None),
    )
    out_specs = (P(("grp", "gx"), None), P(("grp", "gx"), None), P(("grp", "gx"), None))
    return jax.shard_map(
        per_device, mesh=mesh, in_specs=in_specs, out_specs=out_specs, check_vma=False
    )
```

```python
import math

import jax
import jax.numpy as jnp
from jax import lax
from jax.experimental import pallas as pl
from jax.experimental.pallas import tpu as pltpu
from jax.sharding import PartitionSpec as P

AXIS = "gx"
BF = jnp.bfloat16
F32 = jnp.float32


def gelu_parts(preact):
    value = preact.astype(F32)
    coeff = math.sqrt(2.0 / math.pi)
    inner = coeff * (value + 0.044715 * value * value * value)
    tangent = jnp.tanh(inner)
    activ = 0.5 * value * (1.0 + tangent)
    gelu_slope = 0.5 * (1.0 + tangent) + 0.5 * value * (1.0 - tangent * tangent) * coeff * (
        1.0 + 3.0 * 0.044715 * value * value
    )
    return (activ.astype(BF), gelu_slope)


def contract_last(left, right):
    return lax.dot_general(
        left, right, (((1,), (1,)), ((), ())), preferred_element_type=F32
    )


def contract_first(left, right):
    return lax.dot_general(
        left, right, (((0,), (0,)), ((), ())), preferred_element_type=F32
    )


def coords(d):
    return d // 8, (d // 4) % 2, (d // 2) % 2, d % 2


def index(z, y, x, c):
    return ((z * 2 + y) * 2 + x) * 2 + c


def moved(n, f):
    return [(d, index(*f(*coords(d)))) for d in range(n)]


def pick(array, at, axis):
    return lax.dynamic_index_in_dim(array, at, axis, keepdims=False)


def paired(mine, other, at, axis):
    first = jnp.where(at == 0, mine, other)
    second = jnp.where(at == 0, other, mine)
    return jnp.stack([first, second], axis)


def plain(out_grad, inputs, preact, w_out, w_in):
    n = lax.axis_size(AXIS)
    nz = n // 8
    nl = nz // 2
    me = lax.axis_index(AXIS)
    z, y, x, c = coords(me)
    high, low = z // nl, z % nl
    grad_scale = 1.0 / math.sqrt(out_grad.shape[0] * n)
    tokens, width = out_grad.shape
    hidden = preact.shape[1]
    half = hidden // 2
    rows_out, rows_in = w_out.shape[0], w_in.shape[0]

    along_x = moved(n, lambda z, y, x, c: (z, y, 1 - x, c))
    along_y = moved(n, lambda z, y, x, c: (z, 1 - y, x, c))
    cores = moved(n, lambda z, y, x, c: (z, y, x, 1 - c))

    def send(array, perm):
        return lax.ppermute(array, AXIS, perm)

    def z_perm(k):
        return moved(n, lambda z, y, x, c: (z ^ k, y, x, c))

    def gather_perm(i, j):
        return moved(
            n, lambda z, y, x, c: ((c ^ i) * nl + ((z % nl) ^ j), y, x, z // nl)
        )

    def scatter_perm(i, j):
        return moved(
            n, lambda z, y, x, c: (c * nl + ((z % nl) ^ j), y, x, (z // nl) ^ i)
        )

    pre_split = preact.reshape(tokens, 2, half)
    pre_mine = pick(pre_split, c, 1)
    pre_other = send(pick(pre_split, 1 - c, 1), cores)
    out_grad2 = jnp.concatenate([out_grad, send(out_grad, cores)], 0)
    inputs2 = jnp.concatenate([inputs, send(inputs, cores)], 0)
    pre2 = jnp.concatenate([pre_mine, pre_other], 0)

    parts = [[send(w_out, gather_perm(i, j)) for j in range(nl)] for i in range(2)]
    parts = jnp.stack([jnp.stack(p, 0) for p in parts], 0)
    by_z = jnp.stack(
        [
            jnp.stack([parts[cc ^ high, ll ^ low] for cc in range(2)], 0)
            for ll in range(nl)
        ],
        0,
    )

    def gather_plane(array, cut):
        one, two = jnp.split(array, 2, cut)
        one = paired(one, send(one, along_x), x, 0)
        two = paired(two, send(two, along_y), y, 0)
        one = paired(one, send(one, along_y), y, 0)
        two = paired(two, send(two, along_x), x, 1)
        return jnp.concatenate([one, two], cut + 2)

    w_out2 = gather_plane(by_z, 1).transpose(2, 0, 1, 3, 4, 5).reshape(half, width)

    in_split = w_in.reshape(rows_in, 2, half)
    in_two = paired(pick(in_split, c, 1), send(pick(in_split, 1 - c, 1), cores), c, 0)
    parts = jnp.stack([in_two] + [send(in_two, z_perm(k)) for k in range(1, nz)], 0)
    by_z = jnp.stack([parts[zz ^ z] for zz in range(nz)], 0)
    w_in2 = gather_plane(by_z, 3).transpose(2, 0, 1, 3, 4, 5).reshape(width, half)

    def scatter_plane(total, cut):
        one, two = jnp.split(total, 2, cut)
        one = pick(one, x, 2) + send(pick(one, 1 - x, 2).astype(BF), along_x).astype(F32)
        two = pick(two, y, 1) + send(pick(two, 1 - y, 1).astype(BF), along_y).astype(F32)
        one = pick(one, y, 1) + send(pick(one, 1 - y, 1).astype(BF), along_y).astype(F32)
        two = pick(two, x, 1) + send(pick(two, 1 - x, 1).astype(BF), along_x).astype(F32)
        return jnp.concatenate([one, two], cut - 2)

    activ, slope = gelu_parts(pre2)
    total = contract_first(activ, out_grad2)
    total = total.reshape(nl, 2, 2, 2, rows_out, width)
    total = scatter_plane(total, 3)
    narrow = total.astype(BF)
    w_out_grad = 0.0
    for i in range(2):
        for j in range(nl):
            sent = send(narrow[low ^ j, high ^ i], scatter_perm(i, j)).astype(F32)
            if i == 0 and j == 0:
                sent = jnp.where(c == high, total[low, high], sent)
            w_out_grad = w_out_grad + sent
    w_out_grad = w_out_grad * grad_scale

    act_grad = contract_last(out_grad2, w_out2)
    pre_grad = (act_grad * slope).astype(BF)

    total = contract_first(inputs2, pre_grad)
    total = total.reshape(nz, 2, 2, 2 * rows_in, half)
    total = scatter_plane(total, 4)
    narrow = total.astype(BF)
    own = total[z]
    for k in range(1, nz):
        own = own + send(narrow[z ^ k], z_perm(k)).astype(F32)
    own = (own * grad_scale).reshape(2, rows_in, half)
    w_in_grad = paired(own[c], send(own[1 - c], cores), c, 1).reshape(rows_in, hidden)

    part = contract_last(pre_grad, w_in2)
    input_grad = part[:tokens] + send(part[tokens:], cores)
    return (input_grad, w_out_grad, w_in_grad)


MIB = 1 << 20
ANY = pl.BlockSpec(memory_space=pl.ANY)
VMEM = pl.BlockSpec(memory_space=pltpu.VMEM)
SMEM = pl.BlockSpec(memory_space=pltpu.SMEM)


def shape(dims, kind):
    return jax.ShapeDtypeStruct(dims, kind)


class Order:
    def __init__(self):
        self.after = []

    def __call__(self, outs):
        self.after = [outs[0]]
        return outs


def small(body, where, arrays, outs, after=(), scratch=(), name=None, flops=0):
    skipped = len(after)

    def run(*refs):
        body(*refs[: 1 + len(arrays)], *refs[1 + len(arrays) + skipped :])

    moved_bytes = sum(a.size * a.dtype.itemsize for a in list(arrays) + list(outs))
    return pl.pallas_call(
        run,
        name=name or body.__name__,
        out_shape=outs,
        in_specs=[SMEM] + [VMEM] * len(arrays) + [ANY] * skipped,
        out_specs=[VMEM] * len(outs),
        scratch_shapes=list(scratch),
        compiler_params=pltpu.CompilerParams(vmem_limit_bytes=16 * MIB),
        cost_estimate=pl.CostEstimate(
            flops=flops, bytes_accessed=moved_bytes, transcendentals=0
        ),
    )(where, *arrays, *after)


def pair_kernel(at, in_ref, got_ref, out):
    c = at[3]
    size = out.shape[2]
    out[c] = jnp.where(c == 0, in_ref[:, :size], in_ref[:, size:])
    out[1 - c] = jnp.where(c == 0, got_ref[:, :size], got_ref[:, size:])


def join_kernel(at, own1, got1, own2, got2, one, two):
    x, y = at[2], at[1]
    one[x] = own1[...]
    one[1 - x] = got1[...]
    two[y] = own2[...]
    two[1 - y] = got2[...]


def rows_kernel(at, g00, g01, g10, g11, one, two):
    high, low = at[4], at[5]
    rows = g00.shape[0]
    for cc in range(2):
        from_same = jnp.where(high == cc, g00[...], g10[...])
        from_next = jnp.where(high == cc, g01[...], g11[...])
        part = pl.ds(cc * rows, rows)
        one[part, :] = jnp.where(low == 0, from_same, from_next)
        two[part, :] = jnp.where(low == 0, from_next, from_same)


def columns_kernel(at, mine, g1, g2, g3, one, two):
    z = at[0]
    rows, size = mine.shape[0] * mine.shape[1], one.shape[2]
    for k, got in enumerate((mine, g1, g2, g3)):
        value = got[...].reshape(rows, 2 * size)
        one[z ^ k] = value[:, :size]
        two[z ^ k] = value[:, size:]


def out_total(at, cut, pre, pre_got, grad, grad_got, after):
    tokens, width = grad.shape
    size = pre_got.shape[1] // 8
    rows = size // 2

    def body(at, pre_ref, got_ref, grad_ref, grad2_ref, *refs):
        slope, send, keep, total = refs[-4:]
        t = pl.program_id(0)
        x, y = at[2], at[1]
        activ, slope1 = gelu_parts(pre_ref[...])
        slope[pl.ds(0, tokens), :] = slope1
        value = contract_first(activ, grad_ref[...])
        activ, slope2 = gelu_parts(got_ref[...])
        slope[pl.ds(tokens, tokens), :] = slope2
        value = value + contract_first(activ, grad2_ref[...])
        if cut == 0:
            total[...] = value.reshape(2, rows, width)
            send[0] = total[1 - x].astype(BF)
            keep[0] = total[x]
        else:

            @pl.when(t == y)
            def _():
                keep[...] = value.reshape(2, rows, width)

            @pl.when(t != y)
            def _():
                send[...] = value.astype(BF).reshape(2, rows, width)

    whole = lambda t, at: (0, 0)
    if cut == 0:
        parts = pl.BlockSpec((1, rows, width), lambda t, at: (t, 0, 0))
    else:
        parts = pl.BlockSpec((2, rows, width), lambda t, at: (0, 0, 0))
    return pl.pallas_call(
        body,
        name=f"out_total{cut}",
        grid_spec=pltpu.PrefetchScalarGridSpec(
            num_scalar_prefetch=1,
            grid=(2,),
            in_specs=[
                pl.BlockSpec((tokens, size), lambda t, at: (0, at[3] * 4 + cut * 2 + t)),
                pl.BlockSpec((tokens, size), lambda t, at: (0, at[3] * 4 + cut * 2 + t)),
                pl.BlockSpec((tokens, width), whole),
                pl.BlockSpec((tokens, width), whole),
            ]
            + [ANY] * len(after),
            out_specs=[
                pl.BlockSpec((2 * tokens, size), lambda t, at: (0, t)),
                parts,
                parts,
            ],
            scratch_shapes=[pltpu.VMEM((2, rows, width), F32)],
        ),
        out_shape=[
            shape((2 * tokens, 2 * size), F32),
            shape((2, rows, width), BF),
            shape((2, rows, width), F32),
        ],
        compiler_params=pltpu.CompilerParams(vmem_limit_bytes=(56 if cut == 0 else 24) * MIB),
        cost_estimate=pl.CostEstimate(
            flops=8 * tokens * size * width,
            bytes_accessed=20 * MIB,
            transcendentals=4 * tokens * size,
        ),
    )(at, pre, pre_got, grad, grad_got, *after)


def in_total(at, cut, grad, grad_got, inputs, inputs_got, slope, pieces, nz, after):
    tokens, width = grad.shape
    size = slope.shape[1] // 2
    rows = size // 2
    depth = width // (4 * nz)

    def body(at, grad_ref, grad2_ref, in_ref, in2_ref, slope_ref, mine, other, _, pre_grad, send, keep):
        t = pl.program_id(0)
        x, y = at[2], at[1]
        if cut == 0:
            value = jnp.where(t == y, mine[...], other[...]).reshape(size, width)
        else:
            first, second = mine[t], other[t]
            value = jnp.concatenate(
                [jnp.where(x == 0, first, second), jnp.where(x == 0, second, first)], 0
            )
        totals = 0.0
        for part, (g, i) in enumerate(((grad_ref, in_ref), (grad2_ref, in2_ref))):
            at_rows = pl.ds(part * tokens, tokens)
            act_grad = contract_last(g[...], value)
            pre = (act_grad * slope_ref[at_rows, :]).astype(BF)
            pre_grad[at_rows, :] = pre
            totals = totals + contract_first(i[...], pre)
        parts = totals.reshape(nz, 2, 2, depth, size)
        if cut == 0:
            first, second, bit = parts[:, :, 0], parts[:, :, 1], x
        else:
            first, second, bit = parts[:, 0], parts[:, 1], y
        send[...] = jnp.where(bit == 0, second, first).astype(BF)
        keep[...] = jnp.where(bit == 0, first, second)

    whole = lambda t, at: (0, 0)
    tile = lambda t, at: (0, t)
    piece = pl.BlockSpec((2, rows, width), lambda t, at: (0, 0, 0))
    parts = pl.BlockSpec((nz, 2, depth, size), lambda t, at: (0, 0, 0, t))
    return pl.pallas_call(
        body,
        name=f"in_total{cut}",
        grid_spec=pltpu.PrefetchScalarGridSpec(
            num_scalar_prefetch=1,
            grid=(2,),
            in_specs=[pl.BlockSpec((tokens, width), whole)] * 4
            + [pl.BlockSpec((2 * tokens, size), tile)]
            + [piece] * 2
            + [ANY],
            out_specs=[pl.BlockSpec((2 * tokens, size), tile), parts, parts],
        ),
        out_shape=[
            shape((2 * tokens, 2 * size), BF),
            shape((nz, 2, depth, 2 * size), BF),
            shape((nz, 2, depth, 2 * size), F32),
        ],
        compiler_params=pltpu.CompilerParams(vmem_limit_bytes=24 * MIB),
        cost_estimate=pl.CostEstimate(
            flops=16 * tokens * size * width, bytes_accessed=16 * MIB, transcendentals=0
        ),
    )(at, grad, grad_got, inputs, inputs_got, slope, *pieces, *after)


def input_part(at, part, pre_grads, pieces, nz, after, came=None):
    tokens, size = pre_grads[0].shape[0] // 2, pre_grads[0].shape[1]
    depth = pieces[0].shape[2]
    width = 4 * nz * depth
    steps = 2

    def body(at, g0, g1, a0, a1, b0, b1, *refs):
        out, weight0, weight1 = refs[-3:]
        x, y = at[2], at[1]

        @pl.when(pl.program_id(0) == 0)
        def _():
            for k in range(2):
                weight0[:, y, k] = a0[k]
                weight0[:, 1 - y, k] = a1[k]
                weight1[:, k, x] = b0[k]
                weight1[:, k, 1 - x] = b1[k]

        value = contract_last(g0[...], weight0[...].reshape(width, size))
        value = value + contract_last(g1[...], weight1[...].reshape(width, size))
        out[...] = value if came is None else value + refs[0][...]

    piece = pl.BlockSpec((2, nz, depth, size), lambda t, at: (0, 0, 0, 0))
    rows = pl.BlockSpec((tokens // steps, size), lambda t, at: (part * steps + t, 0))
    out = pl.BlockSpec((tokens // steps, width), lambda t, at: (t, 0))
    added = [] if came is None else [came]
    return pl.pallas_call(
        body,
        name=f"input_part{part}",
        grid_spec=pltpu.PrefetchScalarGridSpec(
            num_scalar_prefetch=1,
            grid=(steps,),
            in_specs=[rows] * 2 + [piece] * 4 + [out] * len(added) + [ANY] * len(after),
            out_specs=out,
            scratch_shapes=[pltpu.VMEM((nz, 2, 2, depth, size), BF)] * 2,
        ),
        out_shape=shape((tokens, width), F32),
        compiler_params=pltpu.CompilerParams(vmem_limit_bytes=24 * MIB),
        cost_estimate=pl.CostEstimate(
            flops=4 * tokens * size * width, bytes_accessed=6 * MIB, transcendentals=0
        ),
    )(at, *pre_grads, *pieces, *added, *after)


def per_device(out_grad, inputs, preact, w_out, w_in):
    n = lax.axis_size(AXIS)
    rows_out, rows_in = w_out.shape[0], w_in.shape[0]
    if n != 32 or rows_out % 16 or (2 * rows_in) % 16 or out_grad.shape[1] % 128:
        return plain(out_grad, inputs, preact, w_out, w_in)
    nz = n // 8
    nl = nz // 2
    me = lax.axis_index(AXIS)
    z, y, x, c = coords(me)
    at = jnp.stack([z, y, x, c, z // nl, z % nl]).astype(jnp.int32)
    grad_scale = 1.0 / math.sqrt(out_grad.shape[0] * n)
    tokens, width = out_grad.shape
    hidden = preact.shape[1]
    half = hidden // 2
    size = half // 2

    along_x = moved(n, lambda z, y, x, c: (z, y, 1 - x, c))
    along_y = moved(n, lambda z, y, x, c: (z, 1 - y, x, c))

    def send(array, perm):
        return lax.ppermute(array, AXIS, perm)

    def z_perm(k, swap=0):
        return moved(n, lambda z, y, x, c: (z ^ k, y, x, c ^ swap))

    def gather_perm(i, j):
        return moved(
            n, lambda z, y, x, c: ((c ^ i) * nl + ((z % nl) ^ j), y, x, z // nl)
        )

    def scatter_perm(i, j):
        return moved(
            n, lambda z, y, x, c: (c * nl + ((z % nl) ^ j), y, x, (z // nl) ^ i)
        )

    order = Order()

    def kernel(body, arrays, outs, scratch=(), name=None, flops=0):
        return order(small(body, at, arrays, outs, order.after, scratch, name, flops))

    pre_got = send(preact, z_perm(0, 1))
    grad_got = send(out_grad, z_perm(0, 1))
    got = [send(w_out, gather_perm(i, j)) for i in range(2) for j in range(2)]
    inputs_got = send(inputs, z_perm(0, 1))
    in_got = send(w_in, z_perm(0, 1))

    slopes, sent, kept = [None] * 2, [None] * 2, [None] * 2

    def out_cut(cut):
        s, o, k = out_total(at, cut, preact, pre_got, out_grad, grad_got, order.after)
        order([o])
        slopes[cut], kept[cut] = s, k
        sent[cut] = send(o, (along_x, along_y)[cut])

    def middle(k, r, next_perm, bit, dim):
        dims = k.shape[:dim] + k.shape[dim + 1 :]

        def body(at, k_ref, r_ref, out, keep):
            b = at[bit]
            spot = (slice(None),) * dim
            out[...] = (k_ref[spot + (1 - b,)] + r_ref[spot + (1 - b,)].astype(F32)).astype(BF)
            keep[...] = k_ref[spot + (b,)] + r_ref[spot + (b,)].astype(F32)

        out, keep = kernel(body, [k, r], [shape(dims, BF), shape(dims, F32)], name=f"middle{dim}{bit}")
        return keep, send(out, next_perm)

    def join(one, one_got, two, two_got):
        pair = shape((2,) + one.shape, BF)
        return kernel(join_kernel, [one, one_got, two, two_got], [pair, pair])

    order.after = [inputs_got]
    out_cut(0)

    (in_two,) = kernel(pair_kernel, [w_in, in_got], [shape((2, rows_in, half), BF)])
    in_z = [send(in_two, z_perm(k)) for k in range(1, nz)]

    rows = shape((2 * rows_out, width), BF)
    one, two = kernel(rows_kernel, got, [rows, rows])
    one_got, two_got = send(one, along_x), send(two, along_y)
    out_cut(1)
    ones, twos = join(one, one_got, two, two_got)
    ones_got, twos_got = send(ones, along_y), send(twos, along_x)

    out_sides = [middle(kept[0], sent[0], along_y, 1, 0), middle(kept[1], sent[1], along_x, 2, 0)]

    spread = shape((nz, 2 * rows_in, size), BF)
    one, two = kernel(columns_kernel, [in_two] + in_z, [spread, spread])
    in_pieces = [one, send(one, along_x), two, send(two, along_y)]

    pre_grads, in_sent, in_kept = [None] * 2, [None] * 2, [None] * 2

    def in_cut(cut, pieces):
        p, o, k = in_total(
            at, cut, out_grad, grad_got, inputs, inputs_got, slopes[cut], pieces, nz, order.after
        )
        order([o])
        pre_grads[cut], in_kept[cut] = p, k
        in_sent[cut] = send(o, (along_x, along_y)[cut])

    in_cut(0, [ones, ones_got])

    def out_parts(at, k1, r1, k2, r2, o00, o01, o10, o11, own, total):
        high, low = at[4], at[5]
        total[0] = (k1[...] + r1[...].astype(F32)).reshape(2, rows_out, width)
        total[1] = (k2[...] + r2[...].astype(F32)).reshape(2, rows_out, width)
        own[...] = total[low, high]
        o00[...] = total[low, high].astype(BF)
        o01[...] = total[1 - low, high].astype(BF)
        o10[...] = total[low, 1 - high].astype(BF)
        o11[...] = total[1 - low, 1 - high].astype(BF)

    row = (rows_out, width)
    *out_got, out_own = kernel(
        out_parts,
        [*out_sides[0], *out_sides[1]],
        [shape(row, BF)] * 4 + [shape(row, F32)],
        [pltpu.VMEM((2, 2, rows_out, width), F32)],
    )
    out_got = [send(p, scatter_perm(*divmod(k, 2))) for k, p in enumerate(out_got)]

    in_cut(1, [twos, twos_got])

    one, one_got = middle(in_kept[0], in_sent[0], along_y, 1, 1)
    two, two_got = middle(in_kept[1], in_sent[1], along_x, 2, 1)

    def out_sum(at, own, r00, r01, r10, r11, out):
        first = jnp.where(at[3] == at[4], own[...], r00[...].astype(F32))
        rest = r01[...].astype(F32) + r10[...].astype(F32) + r11[...].astype(F32)
        out[...] = (first + rest) * grad_scale

    (w_out_grad,) = kernel(out_sum, [out_own] + out_got, [shape(out_own.shape, F32)])

    def in_parts(at, k1, r1, k2, r2, *outs):
        z = at[0]
        *outs, own, total = outs
        total[:, :, :size] = k1[...] + r1[...].astype(F32)
        total[:, :, size:] = k2[...] + r2[...].astype(F32)
        own[...] = total[z]
        for k in range(1, nz):
            outs[k - 1][...] = total[z ^ k].astype(BF)

    row = (2 * rows_in, half)
    *in_got, in_own = kernel(
        in_parts,
        [one, one_got, two, two_got],
        [shape(row, BF)] * (nz - 1) + [shape(row, F32)],
        [pltpu.VMEM((nz, 2 * rows_in, half), F32)],
    )
    in_got = [send(p, z_perm(k)) for p, k in zip(in_got, range(1, nz))]

    ones, twos = join(*in_pieces)
    in_pieces = [ones, send(ones, along_y), twos, send(twos, along_x)]

    (part,) = order([input_part(at, 1, pre_grads, in_pieces, nz, order.after)])
    part_got = send(part, z_perm(0, 1))

    def in_sum(at, own, r1, r2, r3, mine, other):
        total = own[...] + r1[...].astype(F32) + r2[...].astype(F32) + r3[...].astype(F32)
        total = total * grad_scale
        first, second = total[:rows_in], total[rows_in:]
        mine[...] = jnp.where(at[3] == 0, first, second)
        other[...] = jnp.where(at[3] == 0, second, first)

    row = shape((rows_in, half), F32)
    mine, other = kernel(in_sum, [in_own] + in_got, [row, row], flops=10**11)
    other = send(other, z_perm(0, 1))

    def in_join(at, mine, other, out):
        c = at[3]
        out[:, :half] = jnp.where(c == 0, mine[...], other[...])
        out[:, half:] = jnp.where(c == 0, other[...], mine[...])

    (w_in_grad,) = kernel(in_join, [mine, other], [shape((rows_in, hidden), F32)])
    input_grad = input_part(at, 0, pre_grads, in_pieces, nz, order.after, part_got)
    return (input_grad, w_out_grad, w_in_grad)


def solution(mesh):
    in_specs = (
        P(("grp", "gx"), None),
        P(("grp", "gx"), None),
        P(("grp", "gx"), None),
        P("gx", None),
        P("gx", None),
    )
    out_specs = (P(("grp", "gx"), None), P(("grp", "gx"), None), P(("grp", "gx"), None))
    return jax.shard_map(
        per_device, mesh=mesh, in_specs=in_specs, out_specs=out_specs, check_vma=False
    )
```

```python
import math

import jax
import jax.numpy as jnp
from jax import lax
from jax.experimental import pallas as pl
from jax.experimental.pallas import tpu as pltpu
from jax.sharding import PartitionSpec as P

AXIS = "gx"
BF = jnp.bfloat16
F32 = jnp.float32


def gelu_parts(preact):
    value = preact.astype(F32)
    coeff = math.sqrt(2.0 / math.pi)
    inner = coeff * (value + 0.044715 * value * value * value)
    tangent = jnp.tanh(inner)
    activ = 0.5 * value * (1.0 + tangent)
    gelu_slope = 0.5 * (1.0 + tangent) + 0.5 * value * (1.0 - tangent * tangent) * coeff * (
        1.0 + 3.0 * 0.044715 * value * value
    )
    return (activ.astype(BF), gelu_slope)


def contract_last(left, right):
    return lax.dot_general(
        left, right, (((1,), (1,)), ((), ())), preferred_element_type=F32
    )


def contract_first(left, right):
    return lax.dot_general(
        left, right, (((0,), (0,)), ((), ())), preferred_element_type=F32
    )


def coords(d):
    return d // 8, (d // 4) % 2, (d // 2) % 2, d % 2


def index(z, y, x, c):
    return ((z * 2 + y) * 2 + x) * 2 + c


def moved(n, f):
    return [(d, index(*f(*coords(d)))) for d in range(n)]


def pick(array, at, axis):
    return lax.dynamic_index_in_dim(array, at, axis, keepdims=False)


def paired(mine, other, at, axis):
    first = jnp.where(at == 0, mine, other)
    second = jnp.where(at == 0, other, mine)
    return jnp.stack([first, second], axis)


def plain(out_grad, inputs, preact, w_out, w_in):
    n = lax.axis_size(AXIS)
    nz = n // 8
    nl = nz // 2
    me = lax.axis_index(AXIS)
    z, y, x, c = coords(me)
    high, low = z // nl, z % nl
    grad_scale = 1.0 / math.sqrt(out_grad.shape[0] * n)
    tokens, width = out_grad.shape
    hidden = preact.shape[1]
    half = hidden // 2
    rows_out, rows_in = w_out.shape[0], w_in.shape[0]

    along_x = moved(n, lambda z, y, x, c: (z, y, 1 - x, c))
    along_y = moved(n, lambda z, y, x, c: (z, 1 - y, x, c))
    cores = moved(n, lambda z, y, x, c: (z, y, x, 1 - c))

    def send(array, perm):
        return lax.ppermute(array, AXIS, perm)

    def z_perm(k):
        return moved(n, lambda z, y, x, c: (z ^ k, y, x, c))

    def gather_perm(i, j):
        return moved(
            n, lambda z, y, x, c: ((c ^ i) * nl + ((z % nl) ^ j), y, x, z // nl)
        )

    def scatter_perm(i, j):
        return moved(
            n, lambda z, y, x, c: (c * nl + ((z % nl) ^ j), y, x, (z // nl) ^ i)
        )

    pre_split = preact.reshape(tokens, 2, half)
    pre_mine = pick(pre_split, c, 1)
    pre_other = send(pick(pre_split, 1 - c, 1), cores)
    out_grad2 = jnp.concatenate([out_grad, send(out_grad, cores)], 0)
    inputs2 = jnp.concatenate([inputs, send(inputs, cores)], 0)
    pre2 = jnp.concatenate([pre_mine, pre_other], 0)

    parts = [[send(w_out, gather_perm(i, j)) for j in range(nl)] for i in range(2)]
    parts = jnp.stack([jnp.stack(p, 0) for p in parts], 0)
    by_z = jnp.stack(
        [
            jnp.stack([parts[cc ^ high, ll ^ low] for cc in range(2)], 0)
            for ll in range(nl)
        ],
        0,
    )

    def gather_plane(array, cut):
        one, two = jnp.split(array, 2, cut)
        one = paired(one, send(one, along_x), x, 0)
        two = paired(two, send(two, along_y), y, 0)
        one = paired(one, send(one, along_y), y, 0)
        two = paired(two, send(two, along_x), x, 1)
        return jnp.concatenate([one, two], cut + 2)

    w_out2 = gather_plane(by_z, 1).transpose(2, 0, 1, 3, 4, 5).reshape(half, width)

    in_split = w_in.reshape(rows_in, 2, half)
    in_two = paired(pick(in_split, c, 1), send(pick(in_split, 1 - c, 1), cores), c, 0)
    parts = jnp.stack([in_two] + [send(in_two, z_perm(k)) for k in range(1, nz)], 0)
    by_z = jnp.stack([parts[zz ^ z] for zz in range(nz)], 0)
    w_in2 = gather_plane(by_z, 3).transpose(2, 0, 1, 3, 4, 5).reshape(width, half)

    def scatter_plane(total, cut):
        one, two = jnp.split(total, 2, cut)
        one = pick(one, x, 2) + send(pick(one, 1 - x, 2).astype(BF), along_x).astype(F32)
        two = pick(two, y, 1) + send(pick(two, 1 - y, 1).astype(BF), along_y).astype(F32)
        one = pick(one, y, 1) + send(pick(one, 1 - y, 1).astype(BF), along_y).astype(F32)
        two = pick(two, x, 1) + send(pick(two, 1 - x, 1).astype(BF), along_x).astype(F32)
        return jnp.concatenate([one, two], cut - 2)

    activ, slope = gelu_parts(pre2)
    total = contract_first(activ, out_grad2)
    total = total.reshape(nl, 2, 2, 2, rows_out, width)
    total = scatter_plane(total, 3)
    narrow = total.astype(BF)
    w_out_grad = 0.0
    for i in range(2):
        for j in range(nl):
            sent = send(narrow[low ^ j, high ^ i], scatter_perm(i, j)).astype(F32)
            if i == 0 and j == 0:
                sent = jnp.where(c == high, total[low, high], sent)
            w_out_grad = w_out_grad + sent
    w_out_grad = w_out_grad * grad_scale

    act_grad = contract_last(out_grad2, w_out2)
    pre_grad = (act_grad * slope).astype(BF)

    total = contract_first(inputs2, pre_grad)
    total = total.reshape(nz, 2, 2, 2 * rows_in, half)
    total = scatter_plane(total, 4)
    narrow = total.astype(BF)
    own = total[z]
    for k in range(1, nz):
        own = own + send(narrow[z ^ k], z_perm(k)).astype(F32)
    own = (own * grad_scale).reshape(2, rows_in, half)
    w_in_grad = paired(own[c], send(own[1 - c], cores), c, 1).reshape(rows_in, hidden)

    part = contract_last(pre_grad, w_in2)
    input_grad = part[:tokens] + send(part[tokens:], cores)
    return (input_grad, w_out_grad, w_in_grad)


MIB = 1 << 20
ANY = pl.BlockSpec(memory_space=pl.ANY)
VMEM = pl.BlockSpec(memory_space=pltpu.VMEM)
SMEM = pl.BlockSpec(memory_space=pltpu.SMEM)


def shape(dims, kind):
    return jax.ShapeDtypeStruct(dims, kind)


class Order:
    def __init__(self):
        self.after = []

    def __call__(self, outs):
        self.after = [outs[0]]
        return outs


def small(body, where, arrays, outs, after=(), scratch=(), name=None, flops=0):
    skipped = len(after)

    def run(*refs):
        body(*refs[: 1 + len(arrays)], *refs[1 + len(arrays) + skipped :])

    moved_bytes = sum(a.size * a.dtype.itemsize for a in list(arrays) + list(outs))
    return pl.pallas_call(
        run,
        name=name or body.__name__,
        out_shape=outs,
        in_specs=[SMEM] + [VMEM] * len(arrays) + [ANY] * skipped,
        out_specs=[VMEM] * len(outs),
        scratch_shapes=list(scratch),
        compiler_params=pltpu.CompilerParams(vmem_limit_bytes=16 * MIB),
        cost_estimate=pl.CostEstimate(
            flops=flops, bytes_accessed=moved_bytes, transcendentals=0
        ),
    )(where, *arrays, *after)


def pair_kernel(at, in_ref, got_ref, out):
    c = at[3]
    size = out.shape[2]
    out[c] = jnp.where(c == 0, in_ref[:, :size], in_ref[:, size:])
    out[1 - c] = jnp.where(c == 0, got_ref[:, :size], got_ref[:, size:])


def join_kernel(at, own1, got1, own2, got2, one, two):
    x, y = at[2], at[1]
    one[x] = own1[...]
    one[1 - x] = got1[...]
    two[y] = own2[...]
    two[1 - y] = got2[...]


def rows_kernel(at, g00, g01, g10, g11, one, two):
    high, low = at[4], at[5]
    rows = g00.shape[0]
    for cc in range(2):
        from_same = jnp.where(high == cc, g00[...], g10[...])
        from_next = jnp.where(high == cc, g01[...], g11[...])
        part = pl.ds(cc * rows, rows)
        one[part, :] = jnp.where(low == 0, from_same, from_next)
        two[part, :] = jnp.where(low == 0, from_next, from_same)


def columns_kernel(at, mine, g1, g2, g3, one, two):
    z = at[0]
    rows, size = mine.shape[0] * mine.shape[1], one.shape[2]
    for k, got in enumerate((mine, g1, g2, g3)):
        value = got[...].reshape(rows, 2 * size)
        one[z ^ k] = value[:, :size]
        two[z ^ k] = value[:, size:]


def out_total(at, cut, pre, pre_got, grad, grad_got, after):
    tokens, width = grad.shape
    size = pre_got.shape[1] // 8
    rows = size // 2

    def body(at, pre_ref, got_ref, grad_ref, grad2_ref, *refs):
        slope, send, keep, total = refs[-4:]
        t = pl.program_id(0)
        x, y = at[2], at[1]
        activ, slope1 = gelu_parts(pre_ref[...])
        slope[pl.ds(0, tokens), :] = slope1
        value = contract_first(activ, grad_ref[...])
        activ, slope2 = gelu_parts(got_ref[...])
        slope[pl.ds(tokens, tokens), :] = slope2
        value = value + contract_first(activ, grad2_ref[...])
        if cut == 0:
            total[...] = value.reshape(2, rows, width)
            send[0] = total[1 - x].astype(BF)
            keep[0] = total[x]
        else:

            @pl.when(t == y)
            def _():
                keep[...] = value.reshape(2, rows, width)

            @pl.when(t != y)
            def _():
                send[...] = value.astype(BF).reshape(2, rows, width)

    whole = lambda t, at: (0, 0)
    if cut == 0:
        parts = pl.BlockSpec((1, rows, width), lambda t, at: (t, 0, 0))
    else:
        parts = pl.BlockSpec((2, rows, width), lambda t, at: (0, 0, 0))
    return pl.pallas_call(
        body,
        name=f"out_total{cut}",
        grid_spec=pltpu.PrefetchScalarGridSpec(
            num_scalar_prefetch=1,
            grid=(2,),
            in_specs=[
                pl.BlockSpec((tokens, size), lambda t, at: (0, at[3] * 4 + cut * 2 + t)),
                pl.BlockSpec((tokens, size), lambda t, at: (0, at[3] * 4 + cut * 2 + t)),
                pl.BlockSpec((tokens, width), whole),
                pl.BlockSpec((tokens, width), whole),
            ]
            + [ANY] * len(after),
            out_specs=[
                pl.BlockSpec((2 * tokens, size), lambda t, at: (0, t)),
                parts,
                parts,
            ],
            scratch_shapes=[pltpu.VMEM((2, rows, width), F32)],
        ),
        out_shape=[
            shape((2 * tokens, 2 * size), F32),
            shape((2, rows, width), BF),
            shape((2, rows, width), F32),
        ],
        compiler_params=pltpu.CompilerParams(vmem_limit_bytes=(56 if cut == 0 else 24) * MIB),
        cost_estimate=pl.CostEstimate(
            flops=8 * tokens * size * width,
            bytes_accessed=20 * MIB,
            transcendentals=4 * tokens * size,
        ),
    )(at, pre, pre_got, grad, grad_got, *after)


def in_total(at, cut, grad, grad_got, inputs, inputs_got, slope, pieces, nz, after):
    tokens, width = grad.shape
    size = slope.shape[1] // 2
    rows = size // 2
    depth = width // (4 * nz)

    def body(at, grad_ref, grad2_ref, in_ref, in2_ref, slope_ref, mine, other, _, pre_grad, send, keep):
        t = pl.program_id(0)
        x, y = at[2], at[1]
        if cut == 0:
            value = jnp.where(t == y, mine[...], other[...]).reshape(size, width)
        else:
            first, second = mine[t], other[t]
            value = jnp.concatenate(
                [jnp.where(x == 0, first, second), jnp.where(x == 0, second, first)], 0
            )
        totals = 0.0
        for part, (g, i) in enumerate(((grad_ref, in_ref), (grad2_ref, in2_ref))):
            at_rows = pl.ds(part * tokens, tokens)
            act_grad = contract_last(g[...], value)
            pre = (act_grad * slope_ref[at_rows, :]).astype(BF)
            pre_grad[at_rows, :] = pre
            totals = totals + contract_first(i[...], pre)
        parts = totals.reshape(nz, 2, 2, depth, size)
        if cut == 0:
            first, second, bit = parts[:, :, 0], parts[:, :, 1], x
        else:
            first, second, bit = parts[:, 0], parts[:, 1], y
        send[...] = jnp.where(bit == 0, second, first).astype(BF)
        keep[...] = jnp.where(bit == 0, first, second)

    whole = lambda t, at: (0, 0)
    tile = lambda t, at: (0, t)
    piece = pl.BlockSpec((2, rows, width), lambda t, at: (0, 0, 0))
    parts = pl.BlockSpec((nz, 2, depth, size), lambda t, at: (0, 0, 0, t))
    return pl.pallas_call(
        body,
        name=f"in_total{cut}",
        grid_spec=pltpu.PrefetchScalarGridSpec(
            num_scalar_prefetch=1,
            grid=(2,),
            in_specs=[pl.BlockSpec((tokens, width), whole)] * 4
            + [pl.BlockSpec((2 * tokens, size), tile)]
            + [piece] * 2
            + [ANY],
            out_specs=[pl.BlockSpec((2 * tokens, size), tile), parts, parts],
        ),
        out_shape=[
            shape((2 * tokens, 2 * size), BF),
            shape((nz, 2, depth, 2 * size), BF),
            shape((nz, 2, depth, 2 * size), F32),
        ],
        compiler_params=pltpu.CompilerParams(vmem_limit_bytes=24 * MIB),
        cost_estimate=pl.CostEstimate(
            flops=16 * tokens * size * width, bytes_accessed=16 * MIB, transcendentals=0
        ),
    )(at, grad, grad_got, inputs, inputs_got, slope, *pieces, *after)


def input_part(at, part, pre_grads, pieces, nz, after, came=None):
    tokens, size = pre_grads[0].shape[0] // 2, pre_grads[0].shape[1]
    depth = pieces[0].shape[2]
    width = 4 * nz * depth
    steps = 2

    def body(at, g0, g1, a0, a1, b0, b1, *refs):
        out, weight0, weight1 = refs[-3:]
        x, y = at[2], at[1]

        @pl.when(pl.program_id(0) == 0)
        def _():
            for k in range(2):
                weight0[:, y, k] = a0[k]
                weight0[:, 1 - y, k] = a1[k]
                weight1[:, k, x] = b0[k]
                weight1[:, k, 1 - x] = b1[k]

        value = contract_last(g0[...], weight0[...].reshape(width, size))
        value = value + contract_last(g1[...], weight1[...].reshape(width, size))
        out[...] = value if came is None else value + refs[0][...]

    piece = pl.BlockSpec((2, nz, depth, size), lambda t, at: (0, 0, 0, 0))
    rows = pl.BlockSpec((tokens // steps, size), lambda t, at: (part * steps + t, 0))
    out = pl.BlockSpec((tokens // steps, width), lambda t, at: (t, 0))
    added = [] if came is None else [came]
    return pl.pallas_call(
        body,
        name=f"input_part{part}",
        grid_spec=pltpu.PrefetchScalarGridSpec(
            num_scalar_prefetch=1,
            grid=(steps,),
            in_specs=[rows] * 2 + [piece] * 4 + [out] * len(added) + [ANY] * len(after),
            out_specs=out,
            scratch_shapes=[pltpu.VMEM((nz, 2, 2, depth, size), BF)] * 2,
        ),
        out_shape=shape((tokens, width), F32),
        compiler_params=pltpu.CompilerParams(vmem_limit_bytes=24 * MIB),
        cost_estimate=pl.CostEstimate(
            flops=4 * tokens * size * width, bytes_accessed=6 * MIB, transcendentals=0
        ),
    )(at, *pre_grads, *pieces, *added, *after)


def per_device(out_grad, inputs, preact, w_out, w_in):
    n = lax.axis_size(AXIS)
    rows_out, rows_in = w_out.shape[0], w_in.shape[0]
    if n != 32 or rows_out % 16 or (2 * rows_in) % 16 or out_grad.shape[1] % 128:
        return plain(out_grad, inputs, preact, w_out, w_in)
    nz = n // 8
    nl = nz // 2
    me = lax.axis_index(AXIS)
    z, y, x, c = coords(me)
    at = jnp.stack([z, y, x, c, z // nl, z % nl]).astype(jnp.int32)
    grad_scale = 1.0 / math.sqrt(out_grad.shape[0] * n)
    tokens, width = out_grad.shape
    hidden = preact.shape[1]
    half = hidden // 2
    size = half // 2

    along_x = moved(n, lambda z, y, x, c: (z, y, 1 - x, c))
    along_y = moved(n, lambda z, y, x, c: (z, 1 - y, x, c))

    def send(array, perm):
        return lax.ppermute(array, AXIS, perm)

    def z_perm(k, swap=0):
        return moved(n, lambda z, y, x, c: (z ^ k, y, x, c ^ swap))

    def gather_perm(i, j):
        return moved(
            n, lambda z, y, x, c: ((c ^ i) * nl + ((z % nl) ^ j), y, x, z // nl)
        )

    def scatter_perm(i, j):
        return moved(
            n, lambda z, y, x, c: (c * nl + ((z % nl) ^ j), y, x, (z // nl) ^ i)
        )

    order = Order()

    def kernel(body, arrays, outs, scratch=(), name=None, flops=0):
        return order(small(body, at, arrays, outs, order.after, scratch, name, flops))

    pre_got = send(preact, z_perm(0, 1))
    grad_got = send(out_grad, z_perm(0, 1))
    got = [send(w_out, gather_perm(i, j)) for i in range(2) for j in range(2)]
    inputs_got = send(inputs, z_perm(0, 1))
    in_got = send(w_in, z_perm(0, 1))

    slopes, sent, kept = [None] * 2, [None] * 2, [None] * 2

    def out_cut(cut):
        s, o, k = out_total(at, cut, preact, pre_got, out_grad, grad_got, order.after)
        order([o])
        slopes[cut], kept[cut] = s, k
        sent[cut] = send(o, (along_x, along_y)[cut])

    def middle(k, r, next_perm, bit, dim):
        dims = k.shape[:dim] + k.shape[dim + 1 :]

        def body(at, k_ref, r_ref, out, keep):
            b = at[bit]
            spot = (slice(None),) * dim
            out[...] = (k_ref[spot + (1 - b,)] + r_ref[spot + (1 - b,)].astype(F32)).astype(BF)
            keep[...] = k_ref[spot + (b,)] + r_ref[spot + (b,)].astype(F32)

        out, keep = kernel(body, [k, r], [shape(dims, BF), shape(dims, F32)], name=f"middle{dim}{bit}")
        return keep, send(out, next_perm)

    def join(one, one_got, two, two_got):
        pair = shape((2,) + one.shape, BF)
        return kernel(join_kernel, [one, one_got, two, two_got], [pair, pair])

    order.after = [inputs_got]
    out_cut(0)

    (in_two,) = kernel(pair_kernel, [w_in, in_got], [shape((2, rows_in, half), BF)])
    in_z = [send(in_two, z_perm(k)) for k in range(1, nz)]

    rows = shape((2 * rows_out, width), BF)
    one, two = kernel(rows_kernel, got, [rows, rows])
    one_got, two_got = send(one, along_x), send(two, along_y)
    out_cut(1)
    ones, twos = join(one, one_got, two, two_got)
    ones_got, twos_got = send(ones, along_y), send(twos, along_x)

    out_sides = [middle(kept[0], sent[0], along_y, 1, 0), middle(kept[1], sent[1], along_x, 2, 0)]

    spread = shape((nz, 2 * rows_in, size), BF)
    one, two = kernel(columns_kernel, [in_two] + in_z, [spread, spread])
    in_pieces = [one, send(one, along_x), two, send(two, along_y)]

    pre_grads, in_sent, in_kept = [None] * 2, [None] * 2, [None] * 2

    def in_cut(cut, pieces):
        p, o, k = in_total(
            at, cut, out_grad, grad_got, inputs, inputs_got, slopes[cut], pieces, nz, order.after
        )
        order([o])
        pre_grads[cut], in_kept[cut] = p, k
        in_sent[cut] = send(o, (along_x, along_y)[cut])

    in_cut(0, [ones, ones_got])

    def out_parts(at, k1, r1, k2, r2, o0, o1, own, total):
        high = at[4]
        total[0] = (k1[...] + r1[...].astype(F32)).reshape(2, rows_out, width)
        total[1] = (k2[...] + r2[...].astype(F32)).reshape(2, rows_out, width)
        own[...] = total[:, high]
        o0[...] = total[:, high].astype(BF)
        o1[...] = total[:, 1 - high].astype(BF)

    both = (2, rows_out, width)
    *out_got, out_own = kernel(
        out_parts,
        [*out_sides[0], *out_sides[1]],
        [shape(both, BF)] * 2 + [shape(both, F32)],
        [pltpu.VMEM((2, 2, rows_out, width), F32)],
    )
    out_got = [send(p, scatter_perm(i, 0)) for i, p in enumerate(out_got)]

    in_cut(1, [twos, twos_got])

    one, one_got = middle(in_kept[0], in_sent[0], along_y, 1, 1)
    two, two_got = middle(in_kept[1], in_sent[1], along_x, 2, 1)

    def out_middle(at, own, r0, r1, out, keep, total):
        high, low = at[4], at[5]
        total[...] = jnp.where(at[3] == high, own[...], r0[...].astype(F32)) + r1[...].astype(F32)
        out[...] = total[1 - low].astype(BF)
        keep[...] = total[low]

    row = (rows_out, width)
    out_got, out_own = kernel(
        out_middle,
        [out_own] + out_got,
        [shape(row, BF), shape(row, F32)],
        [pltpu.VMEM(both, F32)],
    )
    out_got = send(out_got, z_perm(1))


    def in_parts(at, k1, r1, k2, r2, *outs):
        z = at[0]
        *outs, own, total = outs
        total[:, :, :size] = k1[...] + r1[...].astype(F32)
        total[:, :, size:] = k2[...] + r2[...].astype(F32)
        own[...] = total[z]
        for k in range(1, nz):
            outs[k - 1][...] = total[z ^ k].astype(BF)

    row = (2 * rows_in, half)
    *in_got, in_own = kernel(
        in_parts,
        [one, one_got, two, two_got],
        [shape(row, BF)] * (nz - 1) + [shape(row, F32)],
        [pltpu.VMEM((nz, 2 * rows_in, half), F32)],
    )
    in_got = [send(p, z_perm(k)) for p, k in zip(in_got, range(1, nz))]

    def out_sum(at, own, got, out):
        out[...] = (own[...] + got[...].astype(F32)) * grad_scale

    (w_out_grad,) = kernel(out_sum, [out_own, out_got], [shape(out_own.shape, F32)])

    ones, twos = join(*in_pieces)
    in_pieces = [ones, send(ones, along_y), twos, send(twos, along_x)]

    (part,) = order([input_part(at, 1, pre_grads, in_pieces, nz, order.after)])
    part_got = send(part, z_perm(0, 1))
    (part_own,) = order([input_part(at, 0, pre_grads, in_pieces, nz, order.after)])

    def in_sum(at, own, r1, r2, r3, mine, other):
        total = own[...] + r1[...].astype(F32) + r2[...].astype(F32) + r3[...].astype(F32)
        total = total * grad_scale
        first, second = total[:rows_in], total[rows_in:]
        mine[...] = jnp.where(at[3] == 0, first, second)
        other[...] = jnp.where(at[3] == 0, second, first)

    row = shape((rows_in, half), F32)
    mine, other = kernel(in_sum, [in_own] + in_got, [row, row], flops=10**11)
    other = send(other, z_perm(0, 1))

    def in_join(at, mine, other, out):
        c = at[3]
        out[:, :half] = jnp.where(c == 0, mine[...], other[...])
        out[:, half:] = jnp.where(c == 0, other[...], mine[...])

    (w_in_grad,) = kernel(in_join, [mine, other], [shape((rows_in, hidden), F32)])
    def input_sum(at, mine, other, out):
        out[...] = mine[...] + other[...]

    (input_grad,) = kernel(input_sum, [part_own, part_got], [shape((tokens, width), F32)])
    return (input_grad, w_out_grad, w_in_grad)


def solution(mesh):
    in_specs = (
        P(("grp", "gx"), None),
        P(("grp", "gx"), None),
        P(("grp", "gx"), None),
        P("gx", None),
        P("gx", None),
    )
    out_specs = (P(("grp", "gx"), None), P(("grp", "gx"), None), P(("grp", "gx"), None))
    return jax.shard_map(
        per_device, mesh=mesh, in_specs=in_specs, out_specs=out_specs, check_vma=False
    )
```

```python
import math

import jax
import jax.numpy as jnp
from jax import lax
from jax.experimental import pallas as pl
from jax.experimental.pallas import tpu as pltpu
from jax.sharding import PartitionSpec as P

AXIS = "gx"
BF = jnp.bfloat16
F32 = jnp.float32


def gelu_parts(preact):
    value = preact.astype(F32)
    coeff = math.sqrt(2.0 / math.pi)
    inner = coeff * (value + 0.044715 * value * value * value)
    tangent = jnp.tanh(inner)
    activ = 0.5 * value * (1.0 + tangent)
    gelu_slope = 0.5 * (1.0 + tangent) + 0.5 * value * (1.0 - tangent * tangent) * coeff * (
        1.0 + 3.0 * 0.044715 * value * value
    )
    return (activ.astype(BF), gelu_slope)


def contract_last(left, right):
    return lax.dot_general(
        left, right, (((1,), (1,)), ((), ())), preferred_element_type=F32
    )


def contract_first(left, right):
    return lax.dot_general(
        left, right, (((0,), (0,)), ((), ())), preferred_element_type=F32
    )


def coords(d):
    return d // 8, (d // 4) % 2, (d // 2) % 2, d % 2


def index(z, y, x, c):
    return ((z * 2 + y) * 2 + x) * 2 + c


def moved(n, f):
    return [(d, index(*f(*coords(d)))) for d in range(n)]


def pick(array, at, axis):
    return lax.dynamic_index_in_dim(array, at, axis, keepdims=False)


def paired(mine, other, at, axis):
    first = jnp.where(at == 0, mine, other)
    second = jnp.where(at == 0, other, mine)
    return jnp.stack([first, second], axis)


def plain(out_grad, inputs, preact, w_out, w_in):
    n = lax.axis_size(AXIS)
    nz = n // 8
    nl = nz // 2
    me = lax.axis_index(AXIS)
    z, y, x, c = coords(me)
    high, low = z // nl, z % nl
    grad_scale = 1.0 / math.sqrt(out_grad.shape[0] * n)
    tokens, width = out_grad.shape
    hidden = preact.shape[1]
    half = hidden // 2
    rows_out, rows_in = w_out.shape[0], w_in.shape[0]

    along_x = moved(n, lambda z, y, x, c: (z, y, 1 - x, c))
    along_y = moved(n, lambda z, y, x, c: (z, 1 - y, x, c))
    cores = moved(n, lambda z, y, x, c: (z, y, x, 1 - c))

    def send(array, perm):
        return lax.ppermute(array, AXIS, perm)

    def z_perm(k):
        return moved(n, lambda z, y, x, c: (z ^ k, y, x, c))

    def gather_perm(i, j):
        return moved(
            n, lambda z, y, x, c: ((c ^ i) * nl + ((z % nl) ^ j), y, x, z // nl)
        )

    def scatter_perm(i, j):
        return moved(
            n, lambda z, y, x, c: (c * nl + ((z % nl) ^ j), y, x, (z // nl) ^ i)
        )

    pre_split = preact.reshape(tokens, 2, half)
    pre_mine = pick(pre_split, c, 1)
    pre_other = send(pick(pre_split, 1 - c, 1), cores)
    out_grad2 = jnp.concatenate([out_grad, send(out_grad, cores)], 0)
    inputs2 = jnp.concatenate([inputs, send(inputs, cores)], 0)
    pre2 = jnp.concatenate([pre_mine, pre_other], 0)

    parts = [[send(w_out, gather_perm(i, j)) for j in range(nl)] for i in range(2)]
    parts = jnp.stack([jnp.stack(p, 0) for p in parts], 0)
    by_z = jnp.stack(
        [
            jnp.stack([parts[cc ^ high, ll ^ low] for cc in range(2)], 0)
            for ll in range(nl)
        ],
        0,
    )

    def gather_plane(array, cut):
        one, two = jnp.split(array, 2, cut)
        one = paired(one, send(one, along_x), x, 0)
        two = paired(two, send(two, along_y), y, 0)
        one = paired(one, send(one, along_y), y, 0)
        two = paired(two, send(two, along_x), x, 1)
        return jnp.concatenate([one, two], cut + 2)

    w_out2 = gather_plane(by_z, 1).transpose(2, 0, 1, 3, 4, 5).reshape(half, width)

    in_split = w_in.reshape(rows_in, 2, half)
    in_two = paired(pick(in_split, c, 1), send(pick(in_split, 1 - c, 1), cores), c, 0)
    parts = jnp.stack([in_two] + [send(in_two, z_perm(k)) for k in range(1, nz)], 0)
    by_z = jnp.stack([parts[zz ^ z] for zz in range(nz)], 0)
    w_in2 = gather_plane(by_z, 3).transpose(2, 0, 1, 3, 4, 5).reshape(width, half)

    def scatter_plane(total, cut):
        one, two = jnp.split(total, 2, cut)
        one = pick(one, x, 2) + send(pick(one, 1 - x, 2).astype(BF), along_x).astype(F32)
        two = pick(two, y, 1) + send(pick(two, 1 - y, 1).astype(BF), along_y).astype(F32)
        one = pick(one, y, 1) + send(pick(one, 1 - y, 1).astype(BF), along_y).astype(F32)
        two = pick(two, x, 1) + send(pick(two, 1 - x, 1).astype(BF), along_x).astype(F32)
        return jnp.concatenate([one, two], cut - 2)

    activ, slope = gelu_parts(pre2)
    total = contract_first(activ, out_grad2)
    total = total.reshape(nl, 2, 2, 2, rows_out, width)
    total = scatter_plane(total, 3)
    narrow = total.astype(BF)
    w_out_grad = 0.0
    for i in range(2):
        for j in range(nl):
            sent = send(narrow[low ^ j, high ^ i], scatter_perm(i, j)).astype(F32)
            if i == 0 and j == 0:
                sent = jnp.where(c == high, total[low, high], sent)
            w_out_grad = w_out_grad + sent
    w_out_grad = w_out_grad * grad_scale

    act_grad = contract_last(out_grad2, w_out2)
    pre_grad = (act_grad * slope).astype(BF)

    total = contract_first(inputs2, pre_grad)
    total = total.reshape(nz, 2, 2, 2 * rows_in, half)
    total = scatter_plane(total, 4)
    narrow = total.astype(BF)
    own = total[z]
    for k in range(1, nz):
        own = own + send(narrow[z ^ k], z_perm(k)).astype(F32)
    own = (own * grad_scale).reshape(2, rows_in, half)
    w_in_grad = paired(own[c], send(own[1 - c], cores), c, 1).reshape(rows_in, hidden)

    part = contract_last(pre_grad, w_in2)
    input_grad = part[:tokens] + send(part[tokens:], cores)
    return (input_grad, w_out_grad, w_in_grad)


MIB = 1 << 20
ANY = pl.BlockSpec(memory_space=pl.ANY)
VMEM = pl.BlockSpec(memory_space=pltpu.VMEM)
SMEM = pl.BlockSpec(memory_space=pltpu.SMEM)


def shape(dims, kind):
    return jax.ShapeDtypeStruct(dims, kind)


class Order:
    def __init__(self):
        self.after = []

    def __call__(self, outs):
        self.after = [outs[0]]
        return outs


def small(body, where, arrays, outs, after=(), scratch=(), name=None, flops=0):
    skipped = len(after)

    def run(*refs):
        body(*refs[: 1 + len(arrays)], *refs[1 + len(arrays) + skipped :])

    moved_bytes = sum(a.size * a.dtype.itemsize for a in list(arrays) + list(outs))
    return pl.pallas_call(
        run,
        name=name or body.__name__,
        out_shape=outs,
        in_specs=[SMEM] + [VMEM] * len(arrays) + [ANY] * skipped,
        out_specs=[VMEM] * len(outs),
        scratch_shapes=list(scratch),
        compiler_params=pltpu.CompilerParams(vmem_limit_bytes=16 * MIB),
        cost_estimate=pl.CostEstimate(
            flops=flops, bytes_accessed=moved_bytes, transcendentals=0
        ),
    )(where, *arrays, *after)


def pair_kernel(at, in_ref, got_ref, out):
    c = at[3]
    size = out.shape[2]
    out[c] = jnp.where(c == 0, in_ref[:, :size], in_ref[:, size:])
    out[1 - c] = jnp.where(c == 0, got_ref[:, :size], got_ref[:, size:])


def join_kernel(at, own1, got1, own2, got2, one, two):
    x, y = at[2], at[1]
    one[x] = own1[...]
    one[1 - x] = got1[...]
    two[y] = own2[...]
    two[1 - y] = got2[...]


def rows_kernel(at, g00, g01, g10, g11, one, two):
    high, low = at[4], at[5]
    rows = g00.shape[0]
    for cc in range(2):
        from_same = jnp.where(high == cc, g00[...], g10[...])
        from_next = jnp.where(high == cc, g01[...], g11[...])
        part = pl.ds(cc * rows, rows)
        one[part, :] = jnp.where(low == 0, from_same, from_next)
        two[part, :] = jnp.where(low == 0, from_next, from_same)


def columns_kernel(at, mine, g1, g2, g3, one, two):
    z = at[0]
    rows, size = mine.shape[0] * mine.shape[1], one.shape[2]
    for k, got in enumerate((mine, g1, g2, g3)):
        value = got[...].reshape(rows, 2 * size)
        one[z ^ k] = value[:, :size]
        two[z ^ k] = value[:, size:]


def out_total(at, cut, pre, pre_got, grad, grad_got, after):
    tokens, width = grad.shape
    size = pre_got.shape[1] // 8
    rows = size // 2

    def body(at, pre_ref, got_ref, grad_ref, grad2_ref, *refs):
        slope, send, keep, total = refs[-4:]
        t = pl.program_id(0)
        x, y = at[2], at[1]
        activ, slope1 = gelu_parts(pre_ref[...])
        slope[pl.ds(0, tokens), :] = slope1
        value = contract_first(activ, grad_ref[...])
        activ, slope2 = gelu_parts(got_ref[...])
        slope[pl.ds(tokens, tokens), :] = slope2
        value = value + contract_first(activ, grad2_ref[...])
        if cut == 0:
            total[...] = value.reshape(2, rows, width)
            send[0] = total[1 - x].astype(BF)
            keep[0] = total[x]
        else:

            @pl.when(t == y)
            def _():
                keep[...] = value.reshape(2, rows, width)

            @pl.when(t != y)
            def _():
                send[...] = value.astype(BF).reshape(2, rows, width)

    whole = lambda t, at: (0, 0)
    if cut == 0:
        parts = pl.BlockSpec((1, rows, width), lambda t, at: (t, 0, 0))
    else:
        parts = pl.BlockSpec((2, rows, width), lambda t, at: (0, 0, 0))
    return pl.pallas_call(
        body,
        name=f"out_total{cut}",
        grid_spec=pltpu.PrefetchScalarGridSpec(
            num_scalar_prefetch=1,
            grid=(2,),
            in_specs=[
                pl.BlockSpec((tokens, size), lambda t, at: (0, at[3] * 4 + cut * 2 + t)),
                pl.BlockSpec((tokens, size), lambda t, at: (0, at[3] * 4 + cut * 2 + t)),
                pl.BlockSpec((tokens, width), whole),
                pl.BlockSpec((tokens, width), whole),
            ]
            + [ANY] * len(after),
            out_specs=[
                pl.BlockSpec((2 * tokens, size), lambda t, at: (0, t)),
                parts,
                parts,
            ],
            scratch_shapes=[pltpu.VMEM((2, rows, width), F32)],
        ),
        out_shape=[
            shape((2 * tokens, 2 * size), F32),
            shape((2, rows, width), BF),
            shape((2, rows, width), F32),
        ],
        compiler_params=pltpu.CompilerParams(vmem_limit_bytes=(56 if cut == 0 else 24) * MIB),
        cost_estimate=pl.CostEstimate(
            flops=8 * tokens * size * width,
            bytes_accessed=20 * MIB,
            transcendentals=4 * tokens * size,
        ),
    )(at, pre, pre_got, grad, grad_got, *after)


def in_total(at, cut, grad, grad_got, inputs, inputs_got, slope, pieces, nz, after):
    tokens, width = grad.shape
    size = slope.shape[1] // 2
    rows = size // 2
    depth = width // (4 * nz)

    def body(at, grad_ref, grad2_ref, in_ref, in2_ref, slope_ref, mine, other, _, pre_grad, send, keep):
        t = pl.program_id(0)
        x, y = at[2], at[1]
        if cut == 0:
            value = jnp.where(t == y, mine[...], other[...]).reshape(size, width)
        else:
            first, second = mine[t], other[t]
            value = jnp.concatenate(
                [jnp.where(x == 0, first, second), jnp.where(x == 0, second, first)], 0
            )
        totals = 0.0
        for part, (g, i) in enumerate(((grad_ref, in_ref), (grad2_ref, in2_ref))):
            at_rows = pl.ds(part * tokens, tokens)
            act_grad = contract_last(g[...], value)
            pre = (act_grad * slope_ref[at_rows, :]).astype(BF)
            pre_grad[at_rows, :] = pre
            totals = totals + contract_first(i[...], pre)
        parts = totals.reshape(nz, 2, 2, depth, size)
        if cut == 0:
            first, second, bit = parts[:, :, 0], parts[:, :, 1], x
        else:
            first, second, bit = parts[:, 0], parts[:, 1], y
        send[...] = jnp.where(bit == 0, second, first).astype(BF)
        keep[...] = jnp.where(bit == 0, first, second)

    whole = lambda t, at: (0, 0)
    tile = lambda t, at: (0, t)
    piece = pl.BlockSpec((2, rows, width), lambda t, at: (0, 0, 0))
    parts = pl.BlockSpec((nz, 2, depth, size), lambda t, at: (0, 0, 0, t))
    return pl.pallas_call(
        body,
        name=f"in_total{cut}",
        grid_spec=pltpu.PrefetchScalarGridSpec(
            num_scalar_prefetch=1,
            grid=(2,),
            in_specs=[pl.BlockSpec((tokens, width), whole)] * 4
            + [pl.BlockSpec((2 * tokens, size), tile)]
            + [piece] * 2
            + [ANY],
            out_specs=[pl.BlockSpec((2 * tokens, size), tile), parts, parts],
        ),
        out_shape=[
            shape((2 * tokens, 2 * size), BF),
            shape((nz, 2, depth, 2 * size), BF),
            shape((nz, 2, depth, 2 * size), F32),
        ],
        compiler_params=pltpu.CompilerParams(vmem_limit_bytes=24 * MIB),
        cost_estimate=pl.CostEstimate(
            flops=16 * tokens * size * width, bytes_accessed=16 * MIB, transcendentals=0
        ),
    )(at, grad, grad_got, inputs, inputs_got, slope, *pieces, *after)


def input_part(at, part, pre_grads, pieces, nz, after, came=None):
    tokens, size = pre_grads[0].shape[0] // 2, pre_grads[0].shape[1]
    depth = pieces[0].shape[2]
    width = 4 * nz * depth
    steps = 2

    def body(at, g0, g1, a0, a1, b0, b1, *refs):
        out, weight0, weight1 = refs[-3:]
        x, y = at[2], at[1]

        @pl.when(pl.program_id(0) == 0)
        def _():
            for k in range(2):
                weight0[:, y, k] = a0[k]
                weight0[:, 1 - y, k] = a1[k]
                weight1[:, k, x] = b0[k]
                weight1[:, k, 1 - x] = b1[k]

        value = contract_last(g0[...], weight0[...].reshape(width, size))
        value = value + contract_last(g1[...], weight1[...].reshape(width, size))
        out[...] = value if came is None else value + refs[0][...]

    piece = pl.BlockSpec((2, nz, depth, size), lambda t, at: (0, 0, 0, 0))
    rows = pl.BlockSpec((tokens // steps, size), lambda t, at: (part * steps + t, 0))
    out = pl.BlockSpec((tokens // steps, width), lambda t, at: (t, 0))
    added = [] if came is None else [came]
    return pl.pallas_call(
        body,
        name=f"input_part{part}",
        grid_spec=pltpu.PrefetchScalarGridSpec(
            num_scalar_prefetch=1,
            grid=(steps,),
            in_specs=[rows] * 2 + [piece] * 4 + [out] * len(added) + [ANY] * len(after),
            out_specs=out,
            scratch_shapes=[pltpu.VMEM((nz, 2, 2, depth, size), BF)] * 2,
        ),
        out_shape=shape((tokens, width), F32),
        compiler_params=pltpu.CompilerParams(vmem_limit_bytes=24 * MIB),
        cost_estimate=pl.CostEstimate(
            flops=4 * tokens * size * width, bytes_accessed=6 * MIB, transcendentals=0
        ),
    )(at, *pre_grads, *pieces, *added, *after)


def per_device(out_grad, inputs, preact, w_out, w_in):
    n = lax.axis_size(AXIS)
    rows_out, rows_in = w_out.shape[0], w_in.shape[0]
    if n != 32 or rows_out % 16 or (2 * rows_in) % 16 or out_grad.shape[1] % 128:
        return plain(out_grad, inputs, preact, w_out, w_in)
    nz = n // 8
    nl = nz // 2
    me = lax.axis_index(AXIS)
    z, y, x, c = coords(me)
    at = jnp.stack([z, y, x, c, z // nl, z % nl]).astype(jnp.int32)
    grad_scale = 1.0 / math.sqrt(out_grad.shape[0] * n)
    tokens, width = out_grad.shape
    hidden = preact.shape[1]
    half = hidden // 2
    size = half // 2

    along_x = moved(n, lambda z, y, x, c: (z, y, 1 - x, c))
    along_y = moved(n, lambda z, y, x, c: (z, 1 - y, x, c))

    def send(array, perm):
        return lax.ppermute(array, AXIS, perm)

    def z_perm(k, swap=0):
        return moved(n, lambda z, y, x, c: (z ^ k, y, x, c ^ swap))

    def gather_perm(i, j):
        return moved(
            n, lambda z, y, x, c: ((c ^ i) * nl + ((z % nl) ^ j), y, x, z // nl)
        )

    def scatter_perm(i, j):
        return moved(
            n, lambda z, y, x, c: (c * nl + ((z % nl) ^ j), y, x, (z // nl) ^ i)
        )

    order = Order()

    def kernel(body, arrays, outs, scratch=(), name=None, flops=0):
        return order(small(body, at, arrays, outs, order.after, scratch, name, flops))

    pre_got = send(preact, z_perm(0, 1))
    grad_got = send(out_grad, z_perm(0, 1))
    got = [send(w_out, gather_perm(i, j)) for i in range(2) for j in range(2)]
    inputs_got = send(inputs, z_perm(0, 1))
    in_got = send(w_in, z_perm(0, 1))

    slopes, sent, kept = [None] * 2, [None] * 2, [None] * 2

    def out_cut(cut):
        s, o, k = out_total(at, cut, preact, pre_got, out_grad, grad_got, order.after)
        order([o])
        slopes[cut], kept[cut] = s, k
        sent[cut] = send(o, (along_x, along_y)[cut])

    def middle(k, r, next_perm, bit, dim):
        dims = k.shape[:dim] + k.shape[dim + 1 :]

        def body(at, k_ref, r_ref, out, keep):
            b = at[bit]
            spot = (slice(None),) * dim
            out[...] = (k_ref[spot + (1 - b,)] + r_ref[spot + (1 - b,)].astype(F32)).astype(BF)
            keep[...] = k_ref[spot + (b,)] + r_ref[spot + (b,)].astype(F32)

        out, keep = kernel(body, [k, r], [shape(dims, BF), shape(dims, F32)], name=f"middle{dim}{bit}")
        return keep, send(out, next_perm)

    def join(one, one_got, two, two_got):
        pair = shape((2,) + one.shape, BF)
        return kernel(join_kernel, [one, one_got, two, two_got], [pair, pair])

    order.after = [inputs_got]
    out_cut(0)

    (in_two,) = kernel(pair_kernel, [w_in, in_got], [shape((2, rows_in, half), BF)])
    in_z = [send(in_two, z_perm(k)) for k in range(1, nz)]

    rows = shape((2 * rows_out, width), BF)
    one, two = kernel(rows_kernel, got, [rows, rows])
    one_got, two_got = send(one, along_x), send(two, along_y)
    out_cut(1)
    ones, twos = join(one, one_got, two, two_got)
    ones_got, twos_got = send(ones, along_y), send(twos, along_x)

    out_sides = [middle(kept[0], sent[0], along_y, 1, 0), middle(kept[1], sent[1], along_x, 2, 0)]

    spread = shape((nz, 2 * rows_in, size), BF)
    one, two = kernel(columns_kernel, [in_two] + in_z, [spread, spread])
    in_pieces = [one, send(one, along_x), two, send(two, along_y)]

    pre_grads, in_sent, in_kept = [None] * 2, [None] * 2, [None] * 2

    def in_cut(cut, pieces):
        p, o, k = in_total(
            at, cut, out_grad, grad_got, inputs, inputs_got, slopes[cut], pieces, nz, order.after
        )
        order([o])
        pre_grads[cut], in_kept[cut] = p, k
        in_sent[cut] = send(o, (along_x, along_y)[cut])

    in_cut(0, [ones, ones_got])

    def out_parts(at, k1, r1, k2, r2, o0, o1, own, total):
        high = at[4]
        total[0] = (k1[...] + r1[...].astype(F32)).reshape(2, rows_out, width)
        total[1] = (k2[...] + r2[...].astype(F32)).reshape(2, rows_out, width)
        own[...] = total[:, high]
        o0[...] = total[:, high].astype(BF)
        o1[...] = total[:, 1 - high].astype(BF)

    both = (2, rows_out, width)
    *out_got, out_own = kernel(
        out_parts,
        [*out_sides[0], *out_sides[1]],
        [shape(both, BF)] * 2 + [shape(both, F32)],
        [pltpu.VMEM((2, 2, rows_out, width), F32)],
    )
    out_got = [send(p, scatter_perm(i, 0)) for i, p in enumerate(out_got)]

    in_cut(1, [twos, twos_got])

    one, one_got = middle(in_kept[0], in_sent[0], along_y, 1, 1)
    two, two_got = middle(in_kept[1], in_sent[1], along_x, 2, 1)

    def out_middle(at, own, r0, r1, out, keep, total):
        high, low = at[4], at[5]
        total[...] = jnp.where(at[3] == high, own[...], r0[...].astype(F32)) + r1[...].astype(F32)
        out[...] = total[1 - low].astype(BF)
        keep[...] = total[low]

    row = (rows_out, width)
    out_got, out_own = kernel(
        out_middle,
        [out_own] + out_got,
        [shape(row, BF), shape(row, F32)],
        [pltpu.VMEM(both, F32)],
    )
    out_got = send(out_got, z_perm(1))


    def in_parts(at, k1, r1, k2, r2, *outs):
        z = at[0]
        *outs, own, total = outs
        total[:, :, :size] = k1[...] + r1[...].astype(F32)
        total[:, :, size:] = k2[...] + r2[...].astype(F32)
        own[...] = total[z]
        for k in range(1, nz):
            outs[k - 1][...] = total[z ^ k].astype(BF)

    row = (2 * rows_in, half)
    *in_got, in_own = kernel(
        in_parts,
        [one, one_got, two, two_got],
        [shape(row, BF)] * (nz - 1) + [shape(row, F32)],
        [pltpu.VMEM((nz, 2 * rows_in, half), F32)],
    )
    in_got = [send(p, z_perm(k)) for p, k in zip(in_got, range(1, nz))]

    def out_sum(at, own, got, out):
        out[...] = (own[...] + got[...].astype(F32)) * grad_scale

    (w_out_grad,) = kernel(out_sum, [out_own, out_got], [shape(out_own.shape, F32)])

    ones, twos = join(*in_pieces)
    in_pieces = [ones, send(ones, along_y), twos, send(twos, along_x)]

    (part,) = order([input_part(at, 1, pre_grads, in_pieces, nz, order.after)])
    part_got = send(part, z_perm(0, 1))
    (part_own,) = order([input_part(at, 0, pre_grads, in_pieces, nz, order.after)])

    def in_sum(at, own, r1, r2, r3, mine, other):
        total = own[...] + r1[...].astype(F32) + r2[...].astype(F32) + r3[...].astype(F32)
        total = total * grad_scale
        first, second = total[:rows_in], total[rows_in:]
        mine[...] = jnp.where(at[3] == 0, first, second)
        other[...] = jnp.where(at[3] == 0, second, first)

    row = shape((rows_in, half), F32)
    mine, other = kernel(in_sum, [in_own] + in_got, [row, row], flops=10**11)
    other = send(other, z_perm(0, 1))

    def in_join(at, mine, other, out):
        c = at[3]
        out[:, :half] = jnp.where(c == 0, mine[...], other[...])
        out[:, half:] = jnp.where(c == 0, other[...], mine[...])

    (w_in_grad,) = kernel(in_join, [mine, other], [shape((rows_in, hidden), F32)])
    def input_sum(at, mine, other, out):
        out[...] = mine[...] + other[...]

    order.after = [mine]
    (input_grad,) = kernel(input_sum, [part_own, part_got], [shape((tokens, width), F32)])
    return (input_grad, w_out_grad, w_in_grad)


def solution(mesh):
    in_specs = (
        P(("grp", "gx"), None),
        P(("grp", "gx"), None),
        P(("grp", "gx"), None),
        P("gx", None),
        P("gx", None),
    )
    out_specs = (P(("grp", "gx"), None), P(("grp", "gx"), None), P(("grp", "gx"), None))
    return jax.shard_map(
        per_device, mesh=mesh, in_specs=in_specs, out_specs=out_specs, check_vma=False
    )
```
